32 devices in a mesh: seq: 8 (over y, x, core), exp: 4 (over z).
Axes of the slice: x: 2, y: 2, z: 4, core: 2. Of those that a mesh axis runs over, the one named last changes fastest.
Arguments:
- residual_in: bfloat16 [2048, 3072], P('seq'), may hold values from -6 to 6
- queries: bfloat16 [2048, 4096], P('seq', 'exp'), may hold values from -6 to 6
- keys: bfloat16 [2048, 4096], P('seq', 'exp'), may hold values from -6 to 6
- values: bfloat16 [2048, 4096], P('seq', 'exp'), may hold values from -6 to 6
- rates: float32 [32], P('exp'), may hold values from 3.0517578e-05 to 0.0333333333, as said below
- doc_lengths: int32 [16], replicated, may hold values from 1 to 1024, 2048 in all
- out_weight: bfloat16 [4096, 3072], P('exp'), may hold values from -0.09375 to 0.09375
- router: bfloat16 [3072, 4], replicated, may hold values from -0.109375 to 0.109375
- gate_weight: bfloat16 [8, 3072, 2560], P('seq', None, 'exp'), may hold values from -0.109375 to 0.109375
- up_weight: bfloat16 [8, 3072, 2560], P('seq', None, 'exp'), may hold values from -0.109375 to 0.109375
- down_weight: bfloat16 [8, 2560, 3072], P('seq', 'exp'), may hold values from -0.078125 to 0.078125
- routes: int32 [2048, 2], P('seq'), may hold values from 0 to 3, all different within a row; in each aligned block of 256 rows (0 to 255, 256 to 511, ...) at most 136 rows name the same one
Outputs:
- mixed: bfloat16 [2048, 3072], P(('seq', 'exp'))
The draws below stay inside these ranges and needn't reach their ends.
Inputs may be any that keep to these rules, and one draw needn't show every extreme that they name: `rates`: each head forgets at its own rate. `doc_lengths`: the lengths sum to 2048; the longest is exactly 1024. `routes`: the two experts of a position differ. In each aligned block of 256 rows no expert is named by more than 136 rows, and in some block one expert is named by exactly 136 rows.
All inputs are finite; a program needn't handle non-finite values.
Results may differ from the reference program's by a relative error of at most 0.014.
Values may be sent and summed in bfloat16 or wider, within the bound.
No kernel may reach another device: no remote copies, remote signals or barrier semaphores. Data moves between devices by JAX's collectives and lax.ppermute only.
A program may use at most 128 MiB of HBM per device.

```python
import math
import jax
import jax.numpy as jnp
import numpy as np
from jax import lax

D = 3072
H = 32
HD = 128
F = 5120
TOK_S = 256
NDOC = 16
EXPERTS = 4
L = 2048
CAP = 136
SLICE = 640


def draw_rates(key, part):
    uniform_part = jax.random.uniform(key, (H,), jnp.float32)
    log_lower = math.log(1.0 / (16.0 * L))
    log_upper = math.log(1.0 / 30.0)
    return jnp.exp(log_lower + (log_upper - log_lower) * uniform_part)


def block_scale(rng, dims, pieces, smallest, largest):
    gain = 1.0
    for axis_at, shards_of in pieces:
        steps = jax.random.uniform(jax.random.fold_in(jax.random.fold_in(rng, 6), axis_at), (shards_of,), jnp.float32, smallest / len(pieces), largest / len(pieces))
        gain = gain * jnp.repeat(jnp.exp(steps), dims[axis_at] // shards_of).reshape((-1,) + (1,) * (len(dims) - 1 - axis_at))
    return gain


def length_profile(number_of, total, bound, slope):
    weights = [(1 << 20) // math.isqrt(grade ** slope) + 1 for grade in range(2, number_of + 1)]
    rest, counts = total - bound - (number_of - 1), [1] * (number_of - 1)
    while rest > 0:
        free = [i for i in range(number_of - 1) if counts[i] < bound]
        mass, remaining = sum([weights[i] for i in free]), rest
        for i in free:
            extra = min(bound - counts[i], max(1, remaining * weights[i] // mass), rest)
            counts[i] = counts[i] + extra
            rest = rest - extra
    return np.array([bound] + counts)


def ragged(key, amount, total, limit, lean):
    if amount == 2:
        one = jax.random.randint(key, (), max(1, total - limit), min(limit, total - 1) + 1)
        return jnp.stack([one, total - one])
    lengths = jnp.asarray(length_profile(amount, total, limit, lean), jnp.int32)
    pairs = (amount - 1) // 2
    source_of, receiver = lengths[1:1 + 2 * pairs:2], lengths[2:2 + 2 * pairs:2]
    margin = jnp.minimum(source_of - 1, limit - receiver)
    moved = jax.random.randint(jax.random.fold_in(key, 1), (pairs,), 0, 1 << 20) % (margin + 1)
    lengths = lengths.at[1:1 + 2 * pairs:2].set(source_of - moved).at[2:2 + 2 * pairs:2].set(receiver + moved)
    return lengths[jax.random.permutation(jax.random.fold_in(key, 2), amount)]


def deal_out(stream_key, own, number, rows, amount, top, reach, slope):
    order = jax.random.permutation(stream_key, amount)
    packed, ordinary = portions_of(amount, rows * top, reach, slope, True), portions_of(amount, rows * top, reach, slope, False)
    places = jnp.arange(amount)

    def named(tallies, turn):
        used = int((tallies > 0).sum())
        fixed = max(1, used // 4)
        shifted = fixed + (places - fixed + turn * (used - fixed)) % max(1, amount - fixed)
        return jnp.zeros((amount,), jnp.int32).at[order[jnp.where(places < fixed, places, shifted)]].set(jnp.asarray(tallies, jnp.int32))

    tallies = jnp.where(number % 4 == 0, named(packed, number // 4), named(ordinary, number - number // 4 - 1))
    mixed = jax.random.permutation(jax.random.fold_in(own, 3), amount)
    giver, sink = mixed[0:amount // 2 * 2:2], mixed[1:amount // 2 * 2:2]
    slack = jnp.minimum(tallies[giver] - 1, reach - tallies[sink]) // 2
    slack = jnp.where((giver == order[0]) | (sink == order[0]) | (tallies[sink] == 0), 0, jnp.maximum(slack, 0))
    shifted = jax.random.randint(jax.random.fold_in(own, 4), (amount // 2,), 0, 1 << 20) % (slack + 1)
    tallies = tallies.at[giver].add(-shifted).at[sink].add(shifted)
    members = jnp.searchsorted(jnp.cumsum(tallies), jnp.arange(rows * top), side="right").astype(jnp.int32)
    listing = members.reshape(top, rows).T
    listing = listing[jax.random.permutation(jax.random.fold_in(own, 1), rows)]
    turn = jax.random.randint(jax.random.fold_in(own, 2), (rows, 1), 0, top)
    return jnp.take_along_axis(listing, (jnp.arange(top)[None, :] + turn) % top, axis=1)


def portions_of(amount, total, most, skew, full):
    weights = [(1 << 20) // math.isqrt(rank ** skew) + 1 for rank in range(1, amount + 1)]
    largest = most if full else min(most, max(-(-total // amount), total * weights[0] // sum(weights)))
    least = 1 if total - largest >= amount - 1 else 0
    given, spare = [largest] + [least] * (amount - 1), total - largest - least * (amount - 1)
    while spare > 0:
        movable = [i for i in range(1, amount) if given[i] < largest] or [i for i in range(1, amount) if given[i] < most]
        mass, budget = sum([weights[i] for i in movable]), spare
        for i in movable:
            addition = min(most - given[i], max(1, budget * weights[i] // mass), spare)
            given[i] = given[i] + addition
            spare = spare - addition
    return np.array(given)


def bell_draw(own_key, shape, scale, bound, pieces=(), kind=jnp.bfloat16):
    entries = jax.random.normal(own_key, shape, jnp.float32) * scale
    if len(pieces) > 0:
        entries = block_scale(own_key, shape, pieces, -0.22, 0.18) * entries
    return jnp.clip(entries, min=-bound, max=bound).astype(kind)


def setup_inputs(seed: int = 0) -> dict:
    arg_keys = jax.random.split(jax.random.key(seed), 13)
    residual_in = bell_draw(arg_keys[0], (L, D), 1.0, 6.0, ((0, 8),))
    queries = bell_draw(arg_keys[1], (L, H * HD), 1.0, 6.0, ((0, 8), (1, 4)))
    keys = bell_draw(arg_keys[2], (L, H * HD), 1.0, 6.0, ((0, 8), (1, 4)))
    values = bell_draw(arg_keys[3], (L, H * HD), 1.0, 6.0, ((0, 8), (1, 4)))
    rates = draw_rates(jax.random.fold_in(arg_keys[12], 71), 0)
    doc_lengths = ragged(arg_keys[5], NDOC, L, L // 2, 2).astype(jnp.int32)
    out_weight = bell_draw(arg_keys[6], (H * HD, D), (H * HD) ** -0.5, 0.09375, ((0, 4),))
    router = bell_draw(arg_keys[7], (D, EXPERTS), D ** -0.5, 0.109375)
    gate_weight = bell_draw(arg_keys[8], (2 * EXPERTS, D, F // 2), D ** -0.5, 0.109375, ((0, 8), (2, 4)))
    up_weight = bell_draw(arg_keys[9], (2 * EXPERTS, D, F // 2), D ** -0.5, 0.109375, ((0, 8), (2, 4)))
    down_weight = bell_draw(arg_keys[10], (2 * EXPERTS, F // 2, D), F ** -0.5, 0.078125, ((0, 8), (1, 4)))
    routes_keys = jax.random.split(jax.random.fold_in(arg_keys[11], 1), L // TOK_S)
    routes_turns = jax.random.permutation(jax.random.fold_in(arg_keys[11], 3), L // TOK_S)
    routes = jax.vmap(lambda own, number: deal_out(jax.random.fold_in(arg_keys[11], 2), own, number, TOK_S, EXPERTS, 2, CAP, 1))(routes_keys, routes_turns).reshape((L, 2))
    return dict(residual_in=residual_in, queries=queries, keys=keys, values=values, rates=rates, doc_lengths=doc_lengths, out_weight=out_weight, router=router, gate_weight=gate_weight, up_weight=up_weight, down_weight=down_weight, routes=routes)


EPSILON = 1e-06

def rms_rows(rows):
    return rows * lax.rsqrt(lax.optimization_barrier(jnp.mean(rows * rows, axis=-1, keepdims=True)) + EPSILON)

def reference(residual_in, queries, keys, values, rates, doc_lengths, out_weight, router, gate_weight, up_weight, down_weight, routes):
    highest = lax.Precision.HIGHEST
    blocks = L // TOK_S
    position = jnp.arange(L, dtype=jnp.int32)
    doc_starts = (jnp.cumsum(doc_lengths) - doc_lengths).astype(jnp.int32)
    doc_of = (lax.optimization_barrier(jnp.sum((doc_starts[None, :] <= position[:, None]).astype(jnp.int32), axis=1)) - 1).astype(jnp.int32)
    local_index = jnp.arange(TOK_S, dtype=jnp.int32)
    query_heads = queries.reshape(blocks, TOK_S, H, HD)
    key_heads = keys.reshape(blocks, TOK_S, H, HD)
    value_heads = values.reshape(blocks, TOK_S, H, HD)
    doc_blocks = doc_of.reshape(blocks, TOK_S)
    same_last = (doc_blocks == doc_blocks[:, -1:]).astype(jnp.float32)
    distance_end = (TOK_S - local_index).astype(jnp.float32)
    end_weight = jnp.exp(-rates[None, None, :] * distance_end[None, :, None]) * same_last[:, :, None]
    weighted_keys = end_weight[:, :, :, None] * key_heads.astype(jnp.float32)
    block_state = jnp.einsum('ctha,cthb->chab', weighted_keys, value_heads.astype(jnp.float32), precision=highest)
    block_base = jnp.arange(blocks, dtype=jnp.int32) * TOK_S
    first_start = lax.optimization_barrier(jnp.max(jnp.where(doc_starts[None, :] <= block_base[:, None], doc_starts[None, :], 0), axis=1))
    block_end = block_base + TOK_S
    block_ids = jnp.arange(blocks, dtype=jnp.int32)
    usable = (block_ids[None, :] < block_ids[:, None]) & (block_end[None, :] - 1 >= first_start[:, None])
    distance = jnp.maximum(block_base[:, None] - block_end[None, :], 0).astype(jnp.float32)
    weight = jnp.where(usable[:, :, None], jnp.exp(-rates[None, None, :] * distance[:, :, None]), 0.0)
    carried = jnp.einsum('cjh,jhab->chab', weight, block_state, precision=highest)
    carried_rounded = carried.astype(jnp.bfloat16)

    def one_block(inputs):
        query_block, key_block, value_block, carry_block, doc_block = inputs
        query_float = query_block.astype(jnp.float32)
        scores = jnp.einsum('thd,uhd->htu', query_float, key_block.astype(jnp.float32))
        lag_steps = local_index[:, None] - local_index[None, :]
        allowed = (lag_steps >= 0) & (doc_block[:, None] == doc_block[None, :])
        decay_mask = jnp.where(allowed[None], jnp.exp(-rates[:, None, None] * jnp.maximum(lag_steps, 0).astype(jnp.float32)[None]), 0.0)
        probs = (scores * decay_mask).astype(jnp.bfloat16)
        inside_term = jnp.einsum('htu,uhd->thd', probs.astype(jnp.float32), value_block.astype(jnp.float32))
        carried_term = jnp.einsum('thd,hde->the', query_float, carry_block.astype(jnp.float32))
        carry_scale = jnp.exp(-rates[None, :] * local_index.astype(jnp.float32)[:, None]) * (doc_block == doc_block[0]).astype(jnp.float32)[:, None]
        heads_raw = inside_term + carried_term * carry_scale[:, :, None]
        return rms_rows(heads_raw).astype(jnp.bfloat16).reshape(TOK_S, H * HD)
    attn = lax.map(one_block, (query_heads, key_heads, value_heads, carried_rounded, doc_blocks)).reshape(L, H * HD)
    hidden = (residual_in.astype(jnp.float32) + jnp.dot(attn, out_weight, preferred_element_type=jnp.float32)).astype(jnp.bfloat16)
    normed = rms_rows(hidden.astype(jnp.float32)).astype(jnp.bfloat16)
    logits = jnp.dot(normed, router, preferred_element_type=jnp.float32)
    picked_logits = jnp.take_along_axis(logits, routes, axis=1)
    route_weight = jax.nn.sigmoid(picked_logits - picked_logits[:, ::-1])
    pair_expert = routes.reshape(blocks, 2 * TOK_S).astype(jnp.int32)
    expert_ids = jnp.arange(EXPERTS, dtype=jnp.int32)
    onehot = (pair_expert[:, :, None] == expert_ids[None, None, :]).astype(jnp.int32)
    rank_before = (jnp.cumsum(onehot, axis=1) - onehot).astype(jnp.int32)
    slot_index = lax.optimization_barrier(jnp.sum(rank_before * onehot, axis=2)).astype(jnp.int32)
    pair_token = (block_base[:, None] + jnp.arange(2 * TOK_S, dtype=jnp.int32)[None, :] // 2).astype(jnp.int32)
    block_grid = jnp.broadcast_to(block_ids[:, None], pair_expert.shape).astype(jnp.int32)
    row_table = jnp.full((EXPERTS, blocks, CAP), L, jnp.int32).at[pair_expert, block_grid, slot_index].set(pair_token)
    padded_rows = jnp.concatenate([normed, jnp.zeros((1, D), jnp.bfloat16)], axis=0)
    gate_pairs = gate_weight.reshape(EXPERTS, 2, D, F // 2)
    up_pairs = up_weight.reshape(EXPERTS, 2, D, F // 2)
    down_pairs = down_weight.reshape(EXPERTS, 2, F // 2, D)

    def one_expert(inputs):
        table_rows, gate_pair, up_pair, down_pair = inputs
        expert_rows = padded_rows[table_rows.reshape(-1)]
        gate_full = jnp.concatenate([gate_pair[0], gate_pair[1]], axis=1)
        up_full = jnp.concatenate([up_pair[0], up_pair[1]], axis=1)
        down_full = jnp.concatenate([down_pair[0], down_pair[1]], axis=0)
        gate_act = jnp.dot(expert_rows, gate_full, preferred_element_type=jnp.float32)
        up_act = jnp.dot(expert_rows, up_full, preferred_element_type=jnp.float32)
        active = (jax.nn.silu(gate_act) * up_act).astype(jnp.bfloat16)
        running = jnp.zeros((expert_rows.shape[0], D), jnp.float32)
        for slice_number in range(F // SLICE):
            term = jnp.dot(active[:, slice_number * SLICE:(slice_number + 1) * SLICE], down_full[slice_number * SLICE:(slice_number + 1) * SLICE], preferred_element_type=jnp.float32)
            rounded = lax.optimization_barrier(term.astype(jnp.bfloat16))
            running = running + rounded.astype(jnp.float32)
        return running
    expert_out = lax.map(one_expert, (row_table, gate_pairs, up_pairs, down_pairs)).reshape(EXPERTS * blocks * CAP, D)
    flat_index = (pair_expert * (blocks * CAP) + block_grid * CAP + slot_index).reshape(-1).astype(jnp.int32)
    gathered = expert_out[flat_index].reshape(L, 2, D)
    expert_mix = lax.optimization_barrier(jnp.sum(gathered * route_weight[:, :, None], axis=1))
    return (hidden.astype(jnp.float32) + expert_mix).astype(jnp.bfloat16)
```

```python
import jax
import jax.numpy as jnp
from jax import lax
from jax.sharding import PartitionSpec as P

EPSILON = 1e-06
BF = jnp.bfloat16
F32 = jnp.float32


def xor_pairs(count, step):
    return [(i, i ^ step) for i in range(count)]


def line_scatter(part, rows_each, count, me):
    def rows(index):
        return lax.dynamic_slice_in_dim(part, jnp.clip(index, 0, count - 1) * rows_each, rows_each, 0)

    from_left = None
    from_right = None
    for step in range(1, count):
        to_right = rows(me + count - step)
        to_left = rows(me - count + step)
        if step > 1:
            to_right = (to_right.astype(F32) + from_left.astype(F32)).astype(BF)
            to_left = (to_left.astype(F32) + from_right.astype(F32)).astype(BF)
        from_left = lax.ppermute(to_right, "exp", [(i, i + 1) for i in range(step)])
        from_right = lax.ppermute(to_left, "exp", [(count - 1 - i, count - 2 - i) for i in range(step)])
    total = rows(me).astype(F32)
    if count > 1:
        total = total + from_left.astype(F32) + from_right.astype(F32)
    return total


def line_gather(own, count, me):
    rows_each = own.shape[0]
    lower = []
    upper = []
    left = own
    right = own
    for step in range(1, count):
        left = lax.ppermute(left, "exp", [(i, i + 1) for i in range(step - 1, count - 1)])
        right = lax.ppermute(right, "exp", [(i + 1, i) for i in range(0, count - step)])
        lower.append(left)
        upper.append(right)
    spread = jnp.concatenate(lower[::-1] + [own] + upper, axis=0)
    return lax.dynamic_slice_in_dim(spread, (count - 1 - me) * rows_each, count * rows_each, 0)


def body(
    residual_in,
    queries,
    keys,
    values,
    rates,
    doc_lengths,
    out_weight,
    router,
    gate_weight,
    up_weight,
    down_weight,
    routes,
):
    highest = lax.Precision.HIGHEST
    seq_count = lax.axis_size("seq")
    exp_count = lax.axis_size("exp")
    seq_index = lax.axis_index("seq")
    exp_index = lax.axis_index("exp")
    chips = seq_count // 2
    chip = seq_index // 2
    core = seq_index % 2
    block_len = queries.shape[0]
    head_count = rates.shape[0]
    head_size = queries.shape[1] // head_count
    width = out_weight.shape[1]
    half = width // 2
    experts = seq_count // 2
    capacity = exp_count * max(1, 2 * block_len // experts * 17 // (16 * exp_count))
    own_count = block_len // exp_count
    local_index = jnp.arange(block_len, dtype=jnp.int32)
    block_base = seq_index * block_len
    position = block_base + local_index
    doc_starts = jnp.cumsum(doc_lengths) - doc_lengths
    doc_of = jnp.sum((doc_starts[None, :] <= position[:, None]).astype(jnp.int32), axis=1) - 1
    query_heads = queries.reshape(block_len, head_count, head_size)
    key_heads = keys.reshape(block_len, head_count, head_size)
    value_heads = values.reshape(block_len, head_count, head_size)

    distance_end = (block_len - local_index).astype(F32)
    same_last = (doc_of == doc_of[-1]).astype(F32)
    end_weight = jnp.exp(-rates[None, :] * distance_end[:, None]) * same_last[:, None]
    weighted_keys = end_weight[:, :, None] * key_heads.astype(F32)
    end_state = jnp.einsum(
        "tha,thb->hab", weighted_keys, value_heads.astype(F32), precision=highest
    ).astype(BF)

    half_heads = head_count // 2
    head_at = core * half_heads
    partner_state = lax.ppermute(end_state, "seq", xor_pairs(seq_count, 1))
    mine = lax.dynamic_slice_in_dim(end_state, head_at, half_heads, 0).astype(F32)
    theirs = lax.dynamic_slice_in_dim(partner_state, head_at, half_heads, 0).astype(F32)
    first_state = jnp.where(core == 0, mine, theirs)
    second_state = jnp.where(core == 0, theirs, mine)
    half_rates = lax.dynamic_slice_in_dim(rates, head_at, half_heads, 0)

    def start_at(where):
        return jnp.max(jnp.where(doc_starts <= where, doc_starts, 0))

    chip_base = chip * 2 * block_len
    block_decay = jnp.exp(-half_rates * float(block_len))
    last_start = start_at(chip_base + 2 * block_len - 1)
    keep_first = jnp.where(last_start <= chip_base + block_len - 1, block_decay, 0.0)
    chip_state = (second_state + keep_first[:, None, None] * first_state).astype(BF)
    base_start = start_at(chip_base)
    carried_first = jnp.zeros_like(first_state)
    for step in range(1, chips):
        other_state = lax.ppermute(chip_state, "seq", xor_pairs(seq_count, 2 * step))
        other = jnp.bitwise_xor(chip, step)
        other_end = (other + 1) * 2 * block_len
        usable = (other < chip) & (other_end - 1 >= base_start)
        distance = jnp.maximum(chip_base - other_end, 0).astype(F32)
        weight = jnp.where(usable, jnp.exp(-half_rates * distance), 0.0)
        carried_first = carried_first + weight[:, None, None] * other_state.astype(F32)
    middle = chip_base + block_len
    middle_start = start_at(middle)
    take_first = (middle - 1 >= middle_start).astype(F32)
    take_carried = jnp.where(chip_base - 1 >= middle_start, block_decay, 0.0)
    carried_second = take_first * first_state + take_carried[:, None, None] * carried_first
    carried_first = carried_first.astype(BF)
    carried_second = carried_second.astype(BF)
    carried_mine = jnp.where(core == 0, carried_first, carried_second)
    carried_other = lax.ppermute(
        jnp.where(core == 0, carried_second, carried_first), "seq", xor_pairs(seq_count, 1)
    )
    carried_rounded = jnp.concatenate(
        [
            jnp.where(core == 0, carried_mine, carried_other),
            jnp.where(core == 0, carried_other, carried_mine),
        ],
        axis=0,
    )

    scores = jnp.einsum("thd,uhd->htu", query_heads, key_heads, preferred_element_type=F32)
    lag_steps = local_index[:, None] - local_index[None, :]
    allowed = (lag_steps >= 0) & (doc_of[:, None] == doc_of[None, :])
    decay_mask = jnp.where(
        allowed[None],
        jnp.exp(-rates[:, None, None] * jnp.maximum(lag_steps, 0).astype(F32)[None]),
        0.0,
    )
    scaled_scores = (scores * decay_mask).astype(BF)
    inside_term = jnp.einsum(
        "htu,uhd->thd", scaled_scores, value_heads, preferred_element_type=F32
    )
    carried_term = jnp.einsum(
        "thd,hde->the", query_heads, carried_rounded, preferred_element_type=F32
    )
    carry_scale = (
        jnp.exp(-rates[None, :] * local_index.astype(F32)[:, None])
        * (doc_of == doc_of[0]).astype(F32)[:, None]
    )
    heads_raw = inside_term + carried_term * carry_scale[:, :, None]
    attention = (
        (heads_raw * lax.rsqrt(jnp.mean(heads_raw * heads_raw, axis=-1, keepdims=True) + EPSILON))
        .astype(BF)
        .reshape(block_len, head_count * head_size)
    )
    partial_value = jnp.dot(attention, out_weight, preferred_element_type=F32).astype(BF)

    own_total = line_scatter(partial_value, own_count, exp_count, exp_index)
    own_residual = lax.dynamic_slice_in_dim(residual_in, exp_index * own_count, own_count, 0)
    own_hidden = (own_residual.astype(F32) + own_total).astype(BF)
    hidden = line_gather(own_hidden, exp_count, exp_index)
    hidden_wide = hidden.astype(F32)
    row_scale = lax.rsqrt(jnp.mean(hidden_wide * hidden_wide, axis=-1, keepdims=True) + EPSILON)
    logits = jnp.dot(hidden, router, preferred_element_type=F32) * row_scale
    expert_ids = jnp.arange(experts, dtype=jnp.int32)
    chosen = routes[:, :, None] == expert_ids[None, None, :]
    route_logits = jnp.sum(jnp.where(chosen, logits[:, None, :], 0.0), axis=2)
    route_weight = jax.nn.sigmoid(route_logits - route_logits[:, ::-1])

    onehot = jnp.sum(chosen.astype(jnp.int32), axis=1)
    before = (local_index[:, None] > local_index[None, :]).astype(BF)
    rank = jnp.dot(before, onehot.astype(BF), preferred_element_type=F32).astype(jnp.int32)
    slot = jnp.sum(jnp.where(chosen, rank[:, None, :], 0), axis=2)
    group = jnp.bitwise_xor(routes, chip)
    place = group * capacity + slot
    slots = experts * capacity
    slot_ids = jnp.arange(slots, dtype=jnp.int32)
    pick = [(place[:, k][:, None] == slot_ids[None, :]).astype(BF) for k in range(2)]
    spread = jnp.transpose(pick[0] + pick[1])

    here = lax.dynamic_slice_in_dim(hidden, core * half, half, 1)
    there = lax.dynamic_slice_in_dim(hidden, (1 - core) * half, half, 1)
    send_here = jnp.dot(spread, here, preferred_element_type=F32).astype(BF)
    send_there = jnp.dot(spread, there, preferred_element_type=F32).astype(BF)
    arrived = []
    for g in range(chips):
        rows = slice(g * capacity, (g + 1) * capacity)
        for b in range(2):
            block = (send_here if b == 0 else send_there)[rows]
            if g or b:
                block = lax.ppermute(block, "seq", xor_pairs(seq_count, 2 * g + b))
            arrived.append(block)
    mine = jnp.concatenate(arrived, axis=0)
    swap = jnp.concatenate([arrived[i ^ 1] for i in range(seq_count)], axis=0)
    theirs = lax.ppermute(swap, "seq", xor_pairs(seq_count, 1))
    received = jnp.concatenate(
        [jnp.where(core == 0, mine, theirs), jnp.where(core == 0, theirs, mine)], axis=1
    )
    received_wide = received.astype(F32)
    in_scale = lax.rsqrt(
        jnp.mean(received_wide * received_wide, axis=-1, keepdims=True) + EPSILON
    )
    gate_act = jnp.dot(received, gate_weight[0], preferred_element_type=F32) * in_scale
    up_act = jnp.dot(received, up_weight[0], preferred_element_type=F32) * in_scale
    active = (jax.nn.silu(gate_act) * up_act).astype(BF)
    partials = jnp.dot(active, down_weight[0], preferred_element_type=F32).astype(BF)

    keep = lax.dynamic_slice_in_dim(partials, core * half, half, 1)
    give = lax.dynamic_slice_in_dim(partials, (1 - core) * half, half, 1)
    give = give.reshape(chips, 2, capacity, half)[:, ::-1].reshape(seq_count * capacity, half)
    got = lax.ppermute(give, "seq", xor_pairs(seq_count, 1))
    sums = (keep.astype(F32) + got.astype(F32)).astype(BF)
    tables = [[], []]
    for g in range(chips):
        for b in range(2):
            i = 2 * g + b
            block = sums[i * capacity : (i + 1) * capacity]
            if i:
                block = lax.ppermute(block, "seq", xor_pairs(seq_count, i))
            tables[b].append(block)
    mixes = []
    for b in range(2):
        table = jnp.concatenate(tables[b], axis=0)
        mix = sum(
            jnp.dot(pick[k], table, preferred_element_type=F32) * route_weight[:, k : k + 1]
            for k in range(2)
        )
        mixes.append(line_scatter(mix.astype(BF), own_count, exp_count, exp_index))
    own_mix = jnp.concatenate(
        [jnp.where(core == 0, mixes[0], mixes[1]), jnp.where(core == 0, mixes[1], mixes[0])],
        axis=1,
    )
    return (own_hidden.astype(F32) + own_mix).astype(BF)


def solution(mesh):
    in_specs = (
        P("seq", None),
        P("seq", "exp"),
        P("seq", "exp"),
        P("seq", "exp"),
        P("exp"),
        P(),
        P("exp", None),
        P(),
        P("seq", None, "exp"),
        P("seq", None, "exp"),
        P("seq", "exp", None),
        P("seq", None),
    )
    out_specs = P(("seq", "exp"), None)
    return jax.shard_map(body, mesh=mesh, in_specs=in_specs, out_specs=out_specs, check_vma=False)
```

```python
import jax
import jax.numpy as jnp
from jax import lax
from jax.sharding import PartitionSpec as P

EPSILON = 1e-06
BF = jnp.bfloat16
F32 = jnp.float32
CHUNKS = 3
CHUNKS_BACK = 2


def xor_pairs(count, step):
    return [(i, i ^ step) for i in range(count)]


def together(values):
    names = list(values)
    joined = lax.optimization_barrier(tuple(values[name] for name in names))
    return dict(zip(names, joined))


def body(
    residual_in,
    queries,
    keys,
    values,
    rates,
    doc_lengths,
    out_weight,
    router,
    gate_weight,
    up_weight,
    down_weight,
    routes,
):
    highest = lax.Precision.HIGHEST
    seq_count = lax.axis_size("seq")
    exp_count = lax.axis_size("exp")
    seq_index = lax.axis_index("seq")
    exp_index = lax.axis_index("exp")
    chips = seq_count // 2
    chip = seq_index // 2
    core = seq_index % 2
    block_len = queries.shape[0]
    head_count = rates.shape[0]
    head_size = queries.shape[1] // head_count
    width = out_weight.shape[1]
    experts = seq_count // 2
    capacity = exp_count * max(1, 2 * block_len // experts * 17 // (16 * exp_count))
    own_count = block_len // exp_count
    local_index = jnp.arange(block_len, dtype=jnp.int32)
    block_base = seq_index * block_len
    position = block_base + local_index
    doc_starts = jnp.cumsum(doc_lengths) - doc_lengths
    doc_of = jnp.sum((doc_starts[None, :] <= position[:, None]).astype(jnp.int32), axis=1) - 1
    query_heads = queries.reshape(block_len, head_count, head_size)
    key_heads = keys.reshape(block_len, head_count, head_size)
    value_heads = values.reshape(block_len, head_count, head_size)

    distance_end = (block_len - local_index).astype(F32)
    same_last = (doc_of == doc_of[-1]).astype(F32)
    end_weight = jnp.exp(-rates[None, :] * distance_end[:, None]) * same_last[:, None]
    weighted_keys = end_weight[:, :, None] * key_heads.astype(F32)
    end_state = jnp.einsum(
        "tha,thb->hab", weighted_keys, value_heads.astype(F32), precision=highest
    ).astype(BF)

    half_heads = head_count // 2
    head_at = core * half_heads
    partner_state = lax.ppermute(end_state, "seq", xor_pairs(seq_count, 1))
    mine = lax.dynamic_slice_in_dim(end_state, head_at, half_heads, 0).astype(F32)
    theirs = lax.dynamic_slice_in_dim(partner_state, head_at, half_heads, 0).astype(F32)
    first_state = jnp.where(core == 0, mine, theirs)
    second_state = jnp.where(core == 0, theirs, mine)
    half_rates = lax.dynamic_slice_in_dim(rates, head_at, half_heads, 0)

    def start_at(where):
        return jnp.max(jnp.where(doc_starts <= where, doc_starts, 0))

    chip_base = chip * 2 * block_len
    block_decay = jnp.exp(-half_rates * float(block_len))
    last_start = start_at(chip_base + 2 * block_len - 1)
    keep_first = jnp.where(last_start <= chip_base + block_len - 1, block_decay, 0.0)
    chip_state = (second_state + keep_first[:, None, None] * first_state).astype(BF)
    base_start = start_at(chip_base)
    carried_first = jnp.zeros_like(first_state)
    for step in range(1, chips):
        other_state = lax.ppermute(chip_state, "seq", xor_pairs(seq_count, 2 * step))
        other = jnp.bitwise_xor(chip, step)
        other_end = (other + 1) * 2 * block_len
        usable = (other < chip) & (other_end - 1 >= base_start)
        distance = jnp.maximum(chip_base - other_end, 0).astype(F32)
        weight = jnp.where(usable, jnp.exp(-half_rates * distance), 0.0)
        carried_first = carried_first + weight[:, None, None] * other_state.astype(F32)
    middle = chip_base + block_len
    middle_start = start_at(middle)
    take_first = (middle - 1 >= middle_start).astype(F32)
    take_carried = jnp.where(chip_base - 1 >= middle_start, block_decay, 0.0)
    carried_second = take_first * first_state + take_carried[:, None, None] * carried_first
    carried_first = carried_first.astype(BF)
    carried_second = carried_second.astype(BF)
    carried_mine = jnp.where(core == 0, carried_first, carried_second)
    carried_other = lax.ppermute(
        jnp.where(core == 0, carried_second, carried_first), "seq", xor_pairs(seq_count, 1)
    )
    carried_rounded = jnp.concatenate(
        [
            jnp.where(core == 0, carried_mine, carried_other),
            jnp.where(core == 0, carried_other, carried_mine),
        ],
        axis=0,
    )

    scores = jnp.einsum("thd,uhd->htu", query_heads, key_heads, preferred_element_type=F32)
    lag_steps = local_index[:, None] - local_index[None, :]
    allowed = (lag_steps >= 0) & (doc_of[:, None] == doc_of[None, :])
    decay_mask = jnp.where(
        allowed[None],
        jnp.exp(-rates[:, None, None] * jnp.maximum(lag_steps, 0).astype(F32)[None]),
        0.0,
    )
    scaled_scores = (scores * decay_mask).astype(BF)
    inside_term = jnp.einsum(
        "htu,uhd->thd", scaled_scores, value_heads, preferred_element_type=F32
    )
    carried_term = jnp.einsum(
        "thd,hde->the", query_heads, carried_rounded, preferred_element_type=F32
    )
    carry_scale = (
        jnp.exp(-rates[None, :] * local_index.astype(F32)[:, None])
        * (doc_of == doc_of[0]).astype(F32)[:, None]
    )
    heads_raw = inside_term + carried_term * carry_scale[:, :, None]
    attention = (
        (heads_raw * lax.rsqrt(jnp.mean(heads_raw * heads_raw, axis=-1, keepdims=True) + EPSILON))
        .astype(BF)
        .reshape(block_len, head_count * head_size)
    )
    expert_ids = jnp.arange(experts, dtype=jnp.int32)
    chosen = routes[:, :, None] == expert_ids[None, None, :]
    onehot = jnp.sum(chosen.astype(jnp.int32), axis=1)
    before = (local_index[:, None] > local_index[None, :]).astype(BF)
    rank = jnp.dot(before, onehot.astype(BF), preferred_element_type=F32).astype(jnp.int32)
    slot = jnp.sum(jnp.where(chosen, rank[:, None, :], 0), axis=2)
    group = jnp.bitwise_xor(routes, chip)
    place = group * capacity + slot
    slots = experts * capacity
    slot_ids = jnp.arange(slots, dtype=jnp.int32)
    pick = [(place[:, k][:, None] == slot_ids[None, :]).astype(BF) for k in range(2)]
    spread = jnp.transpose(pick[0] + pick[1])

    chunks = CHUNKS
    wide = width // chunks
    reach = exp_count // 2
    mirror = jnp.minimum(exp_index, exp_count - 1 - exp_index)
    stages = 2 * reach - 1
    hidden = {}
    total = {}
    mine = {}
    theirs = {}
    gate_act = None
    up_act = None
    in_squares = None

    def project(i):
        cols = slice(i * wide, (i + 1) * wide)
        return jnp.dot(attention, out_weight[:, cols], preferred_element_type=F32).astype(BF)

    part = {0: project(0)}
    for r in range(chunks + stages + 2):
        done = {}
        for side in range(reach - 1):
            inner = r - side
            outer = r - (stages - 1 - side)
            ins = [(side, side + 1), (exp_count - 1 - side, exp_count - 2 - side)]
            outs = [(b, a) for a, b in ins]
            has_in = 0 <= inner < chunks
            has_out = 0 <= outer < chunks
            if not (has_in or has_out):
                continue
            if has_in and has_out:
                load = jnp.where(mirror == side, total.get(inner, part[inner]), hidden[outer])
            else:
                load = total.get(inner, part[inner]) if has_in else hidden[outer]
            done["side", side] = lax.ppermute(
                load, "exp", (ins if has_in else []) + (outs if has_out else [])
            )
        middle = r - (reach - 1)
        if 0 <= middle < chunks:
            done["middle"] = lax.ppermute(
                total.get(middle, part[middle]), "exp", [(reach - 1, reach), (reach, reach - 1)]
            )
        i = r - stages
        if 0 <= i < chunks:
            send = jnp.dot(spread, hidden[i], preferred_element_type=F32).astype(BF)
            done["group", 0] = send[:capacity]
            for g in range(1, chips):
                block = send[g * capacity : (g + 1) * capacity]
                done["group", g] = lax.ppermute(block, "seq", xor_pairs(seq_count, 2 * g))
        i = r - stages - 1
        if 0 <= i < chunks:
            done["theirs"] = lax.ppermute(mine[i], "seq", xor_pairs(seq_count, 1))
        i = r - stages - 2
        if 0 <= i < chunks:
            rows = jnp.concatenate([mine[i], theirs[i]], axis=0)
            squares = jnp.sum(jnp.square(rows.astype(F32)), axis=-1, keepdims=True)
            depth = slice(i * wide, (i + 1) * wide)
            gate_part = jnp.dot(rows, gate_weight[0, depth], preferred_element_type=F32)
            up_part = jnp.dot(rows, up_weight[0, depth], preferred_element_type=F32)
            done["squares"] = squares if i == 0 else in_squares + squares
            done["gate"] = gate_part if i == 0 else gate_act + gate_part
            done["up"] = up_part if i == 0 else up_act + up_part
        if r + 1 < chunks:
            done["part"] = project(r + 1)
        done = together(done)
        if "part" in done:
            part[r + 1] = done["part"]
        for side in range(reach - 1):
            inner = r - side
            outer = r - (stages - 1 - side)
            if 0 <= inner < chunks:
                total[inner] = (part[inner].astype(F32) + done["side", side].astype(F32)).astype(BF)
            if 0 <= outer < chunks:
                hidden[outer] = jnp.where(mirror == side, done["side", side], hidden[outer])
        if 0 <= middle < chunks:
            residual = residual_in[:, middle * wide : (middle + 1) * wide].astype(F32)
            whole = total.get(middle, part[middle]).astype(F32) + done["middle"].astype(F32)
            hidden[middle] = (residual + whole).astype(BF)
        if ("group", 0) in done:
            mine[r - stages] = jnp.concatenate([done["group", g] for g in range(chips)], axis=0)
        if "theirs" in done:
            theirs[r - stages - 1] = done["theirs"]
        if "gate" in done:
            gate_act, up_act, in_squares = done["gate"], done["up"], done["squares"]
    in_scale = lax.rsqrt(in_squares / width + EPSILON)
    active = (jax.nn.silu(gate_act * in_scale) * (up_act * in_scale)).astype(BF)

    hidden = jnp.concatenate([hidden[i] for i in range(chunks)], axis=1)
    squares = jnp.sum(jnp.square(hidden.astype(F32)), axis=-1, keepdims=True)
    row_scale = lax.rsqrt(squares / width + EPSILON)
    logits = jnp.dot(hidden, router, preferred_element_type=F32) * row_scale
    route_logits = jnp.sum(jnp.where(chosen, logits[:, None, :], 0.0), axis=2)
    route_weight = jax.nn.sigmoid(route_logits - route_logits[:, ::-1])
    own_hidden = lax.dynamic_slice_in_dim(hidden, exp_index * own_count, own_count, 0)

    chunks = CHUNKS_BACK
    wide = width // chunks
    sums = {}
    mixes = {}
    own = {}

    def lower(i):
        cols = slice(i * wide, (i + 1) * wide)
        return jnp.dot(active, down_weight[0, :, cols], preferred_element_type=F32).astype(BF)

    def own_rows(value, index):
        return lax.dynamic_slice_in_dim(value, index * own_count, own_count, 0)

    partials = {0: lower(0)}
    for r in range(chunks + 2):
        done = {}
        i = r - 2
        if 0 <= i < chunks:
            for step in range(1, exp_count):
                block = own_rows(mixes[i], jnp.bitwise_xor(exp_index, step))
                done["own", step] = lax.ppermute(block, "exp", xor_pairs(exp_count, step))
        i = r - 1
        if 0 <= i < chunks:
            for g in range(1, chips):
                block = sums[i][g * capacity : (g + 1) * capacity]
                done["table", g] = lax.ppermute(block, "seq", xor_pairs(seq_count, 2 * g))
        if r < chunks:
            done["got"] = lax.ppermute(partials[r][slots:], "seq", xor_pairs(seq_count, 1))
        if r + 1 < chunks:
            done["partials"] = lower(r + 1)
        done = together(done)
        if "partials" in done:
            partials[r + 1] = done["partials"]
        if "got" in done:
            sums[r] = (partials[r][:slots].astype(F32) + done["got"].astype(F32)).astype(BF)
        i = r - 1
        if 0 <= i < chunks:
            table = jnp.concatenate(
                [sums[i][:capacity]] + [done["table", g] for g in range(1, chips)], axis=0
            )
            mixes[i] = sum(
                jnp.dot(pick[k], table, preferred_element_type=F32) * route_weight[:, k : k + 1]
                for k in range(2)
            ).astype(BF)
        i = r - 2
        if 0 <= i < chunks:
            cols = slice(i * wide, (i + 1) * wide)
            whole = own_hidden[:, cols].astype(F32) + own_rows(mixes[i], exp_index).astype(F32)
            for step in range(1, exp_count):
                whole = whole + done["own", step].astype(F32)
            own[i] = whole.astype(BF)
    return jnp.concatenate([own[i] for i in range(chunks)], axis=1)


def solution(mesh):
    in_specs = (
        P("seq", None),
        P("seq", "exp"),
        P("seq", "exp"),
        P("seq", "exp"),
        P("exp"),
        P(),
        P("exp", None),
        P(),
        P("seq", None, "exp"),
        P("seq", None, "exp"),
        P("seq", "exp", None),
        P("seq", None),
    )
    out_specs = P(("seq", "exp"), None)
    return jax.shard_map(body, mesh=mesh, in_specs=in_specs, out_specs=out_specs, check_vma=False)
```

```python
import functools

import jax
import jax.numpy as jnp
from jax import lax
from jax.experimental import pallas as pl
from jax.experimental.pallas import tpu as pltpu
from jax.sharding import PartitionSpec as P

EPSILON = 1e-06
BF = jnp.bfloat16
F32 = jnp.float32
CHUNKS = 3
CHUNKS_BACK = 3


def xor_pairs(count, step):
    return [(i, i ^ step) for i in range(count)]


def dot(a, b):
    return jnp.dot(a, b, preferred_element_type=F32)


def gate_up_kernel(parts, *refs):
    rows = refs[:parts]
    gate_hbm, up_hbm, gate_out, up_out, squares_out, gate_w, up_w, sems = refs[parts:]
    depth = gate_w.shape[0]
    wide = depth // parts
    copies = [
        pltpu.make_async_copy(hbm.at[0, pl.ds(0, depth)], vmem, sems.at[k])
        for k, (hbm, vmem) in enumerate(((gate_hbm, gate_w), (up_hbm, up_w)))
    ]
    for copy in copies:
        copy.start()
    for copy in copies:
        copy.wait()
    tile = rows[0].shape[0] // 2

    def step(t, carry):
        at = pl.ds(pl.multiple_of(t * tile, 16), tile)
        gate = up = squares = None
        for p in range(parts):
            x = rows[p][at, :]
            x_wide = x.astype(F32)
            depths = slice(p * wide, (p + 1) * wide)
            new = (
                dot(x, gate_w[depths, :]),
                dot(x, up_w[depths, :]),
                jnp.sum(x_wide * x_wide, axis=-1, keepdims=True),
            )
            gate, up, squares = new if p == 0 else (gate + new[0], up + new[1], squares + new[2])
        gate_out[at, :] = gate
        up_out[at, :] = up
        squares_out[at, :] = jnp.broadcast_to(squares, (tile, squares_out.shape[1]))
        return carry

    lax.fori_loop(0, 2, step, 0)


def expert_kernel(
    width, rows, gate_in, up_in, squares_in, gate_hbm, up_hbm, down_hbm, *refs
):
    outs = refs[:-5]
    gate_w, up_w, down_w, act, sems = refs[-5:]
    slots, wide = rows.shape
    copies = [
        pltpu.make_async_copy(hbm, vmem, sems.at[k])
        for k, (hbm, vmem) in enumerate(
            (
                (gate_hbm.at[0, pl.ds(width - wide, wide)], gate_w),
                (up_hbm.at[0, pl.ds(width - wide, wide)], up_w),
                (down_hbm.at[0], down_w),
            )
        )
    ]
    for copy in copies:
        copy.start()
    copies[0].wait()
    copies[1].wait()
    tile = slots // 2

    def step(t, carry):
        at = pl.ds(pl.multiple_of(t * tile, 16), tile)
        x = rows[at, :]
        x_wide = x.astype(F32)
        squares = squares_in[at, :1] + jnp.sum(x_wide * x_wide, axis=-1, keepdims=True)
        scale = lax.rsqrt(squares / width + EPSILON)
        gate = (gate_in[at, :] + dot(x, gate_w[...])) * scale
        up = (up_in[at, :] + dot(x, up_w[...])) * scale
        act[at, :] = (gate * (1.0 / (1.0 + jnp.exp(-gate))) * up).astype(BF)
        return carry

    lax.fori_loop(0, 2, step, 0)
    copies[2].wait()
    left = 0
    for out in outs:
        cols = slice(left, left + out.shape[1])
        left += out.shape[1]

        def lower(t, carry, out=out, cols=cols):
            at = pl.ds(pl.multiple_of(t * tile, 16), tile)
            out[at, :] = dot(act[at, :], down_w[:, cols]).astype(BF)
            return carry

        lax.fori_loop(0, 2, lower, 0)


VMEM = pl.BlockSpec(memory_space=pltpu.VMEM)
ANY = pl.BlockSpec(memory_space=pl.ANY)
VMEM_LIMIT = 40 * 1024 * 1024


def gate_up_first(rows, gate_weight, up_weight):
    slots, wide = rows[0].shape
    units = gate_weight.shape[2]
    depth = wide * len(rows)
    return pl.pallas_call(
        functools.partial(gate_up_kernel, len(rows)),
        out_shape=(
            jax.ShapeDtypeStruct((slots, units), F32),
            jax.ShapeDtypeStruct((slots, units), F32),
            jax.ShapeDtypeStruct((slots, 128), F32),
        ),
        in_specs=[VMEM] * len(rows) + [ANY] * 2,
        out_specs=(VMEM,) * 3,
        scratch_shapes=[
            pltpu.VMEM((depth, units), BF),
            pltpu.VMEM((depth, units), BF),
            pltpu.SemaphoreType.DMA((2,)),
        ],
        compiler_params=pltpu.CompilerParams(vmem_limit_bytes=VMEM_LIMIT),
        cost_estimate=pl.CostEstimate(
            flops=4 * slots * depth * units,
            bytes_accessed=4 * depth * units + 2 * slots * depth + 8 * slots * units,
            transcendentals=0,
        ),
    )(*rows, gate_weight, up_weight)


def expert_last(rows, first, gate_weight, up_weight, down_weight, chunks):
    slots, wide = rows.shape
    units, width = down_weight.shape[1:]
    return pl.pallas_call(
        functools.partial(expert_kernel, width),
        out_shape=tuple(jax.ShapeDtypeStruct((slots, width // chunks), BF) for _ in range(chunks)),
        in_specs=[VMEM] * 4 + [ANY] * 3,
        out_specs=(VMEM,) * chunks,
        scratch_shapes=[
            pltpu.VMEM((wide, units), BF),
            pltpu.VMEM((wide, units), BF),
            pltpu.VMEM((units, width), BF),
            pltpu.VMEM((slots, units), BF),
            pltpu.SemaphoreType.DMA((3,)),
        ],
        compiler_params=pltpu.CompilerParams(vmem_limit_bytes=VMEM_LIMIT),
        cost_estimate=pl.CostEstimate(
            flops=4 * slots * wide * units + 2 * slots * units * width,
            bytes_accessed=2 * units * (2 * wide + width) + 2 * slots * (wide + width) + 8 * slots * units,
            transcendentals=slots * units,
        ),
    )(rows, *first, gate_weight, up_weight, down_weight)


def together(values):
    names = list(values)
    joined = lax.optimization_barrier(tuple(values[name] for name in names))
    return dict(zip(names, joined))


def body(
    residual_in,
    queries,
    keys,
    values,
    rates,
    doc_lengths,
    out_weight,
    router,
    gate_weight,
    up_weight,
    down_weight,
    routes,
):
    highest = lax.Precision.HIGHEST
    seq_count = lax.axis_size("seq")
    exp_count = lax.axis_size("exp")
    seq_index = lax.axis_index("seq")
    exp_index = lax.axis_index("exp")
    chips = seq_count // 2
    chip = seq_index // 2
    core = seq_index % 2
    block_len = queries.shape[0]
    head_count = rates.shape[0]
    head_size = queries.shape[1] // head_count
    width = out_weight.shape[1]
    experts = seq_count // 2
    capacity = exp_count * max(1, 2 * block_len // experts * 17 // (16 * exp_count))
    own_count = block_len // exp_count
    local_index = jnp.arange(block_len, dtype=jnp.int32)
    block_base = seq_index * block_len
    position = block_base + local_index
    doc_starts = jnp.cumsum(doc_lengths) - doc_lengths
    doc_of = jnp.sum((doc_starts[None, :] <= position[:, None]).astype(jnp.int32), axis=1) - 1
    query_heads = queries.reshape(block_len, head_count, head_size)
    key_heads = keys.reshape(block_len, head_count, head_size)
    value_heads = values.reshape(block_len, head_count, head_size)

    distance_end = (block_len - local_index).astype(F32)
    same_last = (doc_of == doc_of[-1]).astype(F32)
    end_weight = jnp.exp(-rates[None, :] * distance_end[:, None]) * same_last[:, None]
    weighted_keys = end_weight[:, :, None] * key_heads.astype(F32)
    end_state = jnp.einsum(
        "tha,thb->hab", weighted_keys, value_heads.astype(F32), precision=highest
    ).astype(BF)

    half_heads = head_count // 2
    head_at = core * half_heads
    partner_state = lax.ppermute(end_state, "seq", xor_pairs(seq_count, 1))
    mine = lax.dynamic_slice_in_dim(end_state, head_at, half_heads, 0).astype(F32)
    theirs = lax.dynamic_slice_in_dim(partner_state, head_at, half_heads, 0).astype(F32)
    first_state = jnp.where(core == 0, mine, theirs)
    second_state = jnp.where(core == 0, theirs, mine)
    half_rates = lax.dynamic_slice_in_dim(rates, head_at, half_heads, 0)

    def start_at(where):
        return jnp.max(jnp.where(doc_starts <= where, doc_starts, 0))

    chip_base = chip * 2 * block_len
    block_decay = jnp.exp(-half_rates * float(block_len))
    last_start = start_at(chip_base + 2 * block_len - 1)
    keep_first = jnp.where(last_start <= chip_base + block_len - 1, block_decay, 0.0)
    chip_state = (second_state + keep_first[:, None, None] * first_state).astype(BF)
    base_start = start_at(chip_base)
    carried_first = jnp.zeros_like(first_state)
    for step in range(1, chips):
        other_state = lax.ppermute(chip_state, "seq", xor_pairs(seq_count, 2 * step))
        other = jnp.bitwise_xor(chip, step)
        other_end = (other + 1) * 2 * block_len
        usable = (other < chip) & (other_end - 1 >= base_start)
        distance = jnp.maximum(chip_base - other_end, 0).astype(F32)
        weight = jnp.where(usable, jnp.exp(-half_rates * distance), 0.0)
        carried_first = carried_first + weight[:, None, None] * other_state.astype(F32)
    middle = chip_base + block_len
    middle_start = start_at(middle)
    take_first = (middle - 1 >= middle_start).astype(F32)
    take_carried = jnp.where(chip_base - 1 >= middle_start, block_decay, 0.0)
    carried_second = take_first * first_state + take_carried[:, None, None] * carried_first
    carried_first = carried_first.astype(BF)
    carried_second = carried_second.astype(BF)
    carried_mine = jnp.where(core == 0, carried_first, carried_second)
    carried_other = lax.ppermute(
        jnp.where(core == 0, carried_second, carried_first), "seq", xor_pairs(seq_count, 1)
    )
    carried_rounded = jnp.concatenate(
        [
            jnp.where(core == 0, carried_mine, carried_other),
            jnp.where(core == 0, carried_other, carried_mine),
        ],
        axis=0,
    )

    scores = jnp.einsum("thd,uhd->htu", query_heads, key_heads, preferred_element_type=F32)
    lag_steps = local_index[:, None] - local_index[None, :]
    allowed = (lag_steps >= 0) & (doc_of[:, None] == doc_of[None, :])
    decay_mask = jnp.where(
        allowed[None],
        jnp.exp(-rates[:, None, None] * jnp.maximum(lag_steps, 0).astype(F32)[None]),
        0.0,
    )
    scaled_scores = (scores * decay_mask).astype(BF)
    inside_term = jnp.einsum(
        "htu,uhd->thd", scaled_scores, value_heads, preferred_element_type=F32
    )
    carried_term = jnp.einsum(
        "thd,hde->the", query_heads, carried_rounded, preferred_element_type=F32
    )
    carry_scale = (
        jnp.exp(-rates[None, :] * local_index.astype(F32)[:, None])
        * (doc_of == doc_of[0]).astype(F32)[:, None]
    )
    heads_raw = inside_term + carried_term * carry_scale[:, :, None]
    attention = (
        (heads_raw * lax.rsqrt(jnp.mean(heads_raw * heads_raw, axis=-1, keepdims=True) + EPSILON))
        .astype(BF)
        .reshape(block_len, head_count * head_size)
    )
    expert_ids = jnp.arange(experts, dtype=jnp.int32)
    chosen = routes[:, :, None] == expert_ids[None, None, :]
    onehot = jnp.sum(chosen.astype(jnp.int32), axis=1)
    before = (local_index[:, None] > local_index[None, :]).astype(BF)
    rank = jnp.dot(before, onehot.astype(BF), preferred_element_type=F32).astype(jnp.int32)
    slot = jnp.sum(jnp.where(chosen, rank[:, None, :], 0), axis=2)
    group = jnp.bitwise_xor(routes, chip)
    place = group * capacity + slot
    slots = experts * capacity
    slot_ids = jnp.arange(slots, dtype=jnp.int32)
    pick = [(place[:, k][:, None] == slot_ids[None, :]).astype(BF) for k in range(2)]
    spread = jnp.transpose(pick[0] + pick[1])

    chunks = CHUNKS
    wide = width // chunks
    reach = exp_count // 2
    mirror = jnp.minimum(exp_index, exp_count - 1 - exp_index)
    stages = 2 * reach - 1
    hidden = {}
    total = {}
    mine = {}
    theirs = {}

    def project(i):
        cols = slice(i * wide, (i + 1) * wide)
        return jnp.dot(attention, out_weight[:, cols], preferred_element_type=F32).astype(BF)

    part = {0: project(0)}
    for r in range(chunks + stages + 1):
        done = {}
        for side in range(reach - 1):
            inner = r - side
            outer = r - (stages - 1 - side)
            ins = [(side, side + 1), (exp_count - 1 - side, exp_count - 2 - side)]
            outs = [(b, a) for a, b in ins]
            has_in = 0 <= inner < chunks
            has_out = 0 <= outer < chunks
            if not (has_in or has_out):
                continue
            if has_in and has_out:
                load = jnp.where(mirror == side, total.get(inner, part[inner]), hidden[outer])
            else:
                load = total.get(inner, part[inner]) if has_in else hidden[outer]
            done["side", side] = lax.ppermute(
                load, "exp", (ins if has_in else []) + (outs if has_out else [])
            )
        middle = r - (reach - 1)
        if 0 <= middle < chunks:
            done["middle"] = lax.ppermute(
                total.get(middle, part[middle]), "exp", [(reach - 1, reach), (reach, reach - 1)]
            )
        i = r - stages
        if 0 <= i < chunks:
            send = jnp.dot(spread, hidden[i], preferred_element_type=F32).astype(BF)
            done["group", 0] = send[:capacity]
            for g in range(1, chips):
                block = send[g * capacity : (g + 1) * capacity]
                done["group", g] = lax.ppermute(block, "seq", xor_pairs(seq_count, 2 * g))
        i = r - stages - 1
        if 0 <= i < chunks:
            done["theirs"] = lax.ppermute(mine[i], "seq", xor_pairs(seq_count, 1))
        if r == stages + chunks - 1:
            theirs[chunks - 2] = done["theirs"]
            firsts = {
                "mine": gate_up_first([mine[i] for i in range(chunks - 1)], gate_weight, up_weight),
                "theirs": gate_up_first(
                    [theirs[i] for i in range(chunks - 1)], gate_weight, up_weight
                ),
            }
            for side in firsts:
                for k in range(3):
                    done["first", side, k] = firsts[side][k]
        if r == stages + chunks:
            done["lowered"] = expert_last(
                mine[chunks - 1], firsts["mine"], gate_weight, up_weight, down_weight, CHUNKS_BACK
            )
        if r + 1 < chunks:
            done["part"] = project(r + 1)
        done = together(done)
        if "part" in done:
            part[r + 1] = done["part"]
        for side in range(reach - 1):
            inner = r - side
            outer = r - (stages - 1 - side)
            if 0 <= inner < chunks:
                total[inner] = (part[inner].astype(F32) + done["side", side].astype(F32)).astype(BF)
            if 0 <= outer < chunks:
                hidden[outer] = jnp.where(mirror == side, done["side", side], hidden[outer])
        if 0 <= middle < chunks:
            residual = residual_in[:, middle * wide : (middle + 1) * wide].astype(F32)
            whole = total.get(middle, part[middle]).astype(F32) + done["middle"].astype(F32)
            hidden[middle] = (residual + whole).astype(BF)
        if ("group", 0) in done:
            mine[r - stages] = jnp.concatenate([done["group", g] for g in range(chips)], axis=0)
        if "theirs" in done:
            theirs[r - stages - 1] = done["theirs"]
        if ("first", "mine", 0) in done:
            firsts = {
                side: [done["first", side, k] for k in range(3)] for side in ("mine", "theirs")
            }
    kept = done["lowered"]
    partials = expert_last(
        theirs[chunks - 1], firsts["theirs"], gate_weight, up_weight, down_weight, CHUNKS_BACK
    )

    hidden = jnp.concatenate([hidden[i] for i in range(chunks)], axis=1)
    squares = jnp.sum(jnp.square(hidden.astype(F32)), axis=-1, keepdims=True)
    row_scale = lax.rsqrt(squares / width + EPSILON)
    logits = jnp.dot(hidden, router, preferred_element_type=F32) * row_scale
    route_logits = jnp.sum(jnp.where(chosen, logits[:, None, :], 0.0), axis=2)
    route_weight = jax.nn.sigmoid(route_logits - route_logits[:, ::-1])
    own_hidden = lax.dynamic_slice_in_dim(hidden, exp_index * own_count, own_count, 0)

    chunks = CHUNKS_BACK
    wide = width // chunks
    sums = {}
    mixes = {}
    own = {}

    def own_rows(value, index):
        return lax.dynamic_slice_in_dim(value, index * own_count, own_count, 0)

    for r in range(chunks + 2):
        done = {}
        i = r - 1
        if 0 <= i < chunks:
            for g in range(1, chips):
                block = sums[i][g * capacity : (g + 1) * capacity]
                done["table", g] = lax.ppermute(block, "seq", xor_pairs(seq_count, 2 * g))
        i = r - 2
        if 0 <= i < chunks:
            for step in range(exp_count - 1, 0, -1):
                block = own_rows(mixes[i], jnp.bitwise_xor(exp_index, step))
                done["own", step] = lax.ppermute(block, "exp", xor_pairs(exp_count, step))
        for i in range(chunks):
            if r == min(i, 1):
                done["got", i] = lax.ppermute(partials[i], "seq", xor_pairs(seq_count, 1))
        done = together(done)
        for i in range(chunks):
            if ("got", i) in done:
                sums[i] = (
                    kept[i].astype(F32) + done["got", i].astype(F32)
                ).astype(BF)
        i = r - 1
        if 0 <= i < chunks:
            table = jnp.concatenate(
                [sums[i][:capacity]] + [done["table", g] for g in range(1, chips)], axis=0
            )
            mixes[i] = sum(
                jnp.dot(pick[k], table, preferred_element_type=F32) * route_weight[:, k : k + 1]
                for k in range(2)
            ).astype(BF)
        i = r - 2
        if 0 <= i < chunks:
            cols = slice(i * wide, (i + 1) * wide)
            whole = own_hidden[:, cols].astype(F32) + own_rows(mixes[i], exp_index).astype(F32)
            for step in range(1, exp_count):
                whole = whole + done["own", step].astype(F32)
            own[i] = whole.astype(BF)
    return jnp.concatenate([own[i] for i in range(chunks)], axis=1)


def solution(mesh):
    in_specs = (
        P("seq", None),
        P("seq", "exp"),
        P("seq", "exp"),
        P("seq", "exp"),
        P("exp"),
        P(),
        P("exp", None),
        P(),
        P("seq", None, "exp"),
        P("seq", None, "exp"),
        P("seq", "exp", None),
        P("seq", None),
    )
    out_specs = P(("seq", "exp"), None)
    return jax.shard_map(body, mesh=mesh, in_specs=in_specs, out_specs=out_specs, check_vma=False)
```

```python
import functools

import jax
import jax.numpy as jnp
from jax import lax
from jax.experimental import pallas as pl
from jax.experimental.pallas import tpu as pltpu
from jax.sharding import PartitionSpec as P

EPSILON = 1e-06
BF = jnp.bfloat16
F32 = jnp.float32
CHUNKS = 3
CHUNKS_BACK = 3


def xor_pairs(count, step):
    return [(i, i ^ step) for i in range(count)]


def dot(a, b):
    return jnp.dot(a, b, preferred_element_type=F32)


def gate_up_kernel(parts, *refs):
    rows = refs[:parts]
    gate_hbm, up_hbm, gate_out, up_out, squares_out, gate_w, up_w, sems = refs[parts:]
    depth = gate_w.shape[0]
    wide = depth // parts
    copies = [
        pltpu.make_async_copy(hbm.at[0, pl.ds(0, depth)], vmem, sems.at[k])
        for k, (hbm, vmem) in enumerate(((gate_hbm, gate_w), (up_hbm, up_w)))
    ]
    for copy in copies:
        copy.start()
    for copy in copies:
        copy.wait()
    tile = rows[0].shape[0] // 2

    def step(t, carry):
        at = pl.ds(pl.multiple_of(t * tile, 16), tile)
        gate = up = squares = None
        for p in range(parts):
            x = rows[p][at, :]
            x_wide = x.astype(F32)
            depths = slice(p * wide, (p + 1) * wide)
            new = (
                dot(x, gate_w[depths, :]),
                dot(x, up_w[depths, :]),
                jnp.sum(x_wide * x_wide, axis=-1, keepdims=True),
            )
            gate, up, squares = new if p == 0 else (gate + new[0], up + new[1], squares + new[2])
        gate_out[at, :] = gate
        up_out[at, :] = up
        squares_out[at, :] = jnp.broadcast_to(squares, (tile, squares_out.shape[1]))
        return carry

    lax.fori_loop(0, 2, step, 0)


def expert_kernel(
    width, rows, gate_in, up_in, squares_in, gate_hbm, up_hbm, down_hbm, *refs
):
    outs = refs[:-5]
    gate_w, up_w, down_w, act, sems = refs[-5:]
    slots, wide = rows.shape
    copies = [
        pltpu.make_async_copy(hbm, vmem, sems.at[k])
        for k, (hbm, vmem) in enumerate(
            (
                (gate_hbm.at[0, pl.ds(width - wide, wide)], gate_w),
                (up_hbm.at[0, pl.ds(width - wide, wide)], up_w),
                (down_hbm.at[0], down_w),
            )
        )
    ]
    for copy in copies:
        copy.start()
    copies[0].wait()
    copies[1].wait()
    tile = slots // 2

    def step(t, carry):
        at = pl.ds(pl.multiple_of(t * tile, 16), tile)
        x = rows[at, :]
        x_wide = x.astype(F32)
        squares = squares_in[at, :1] + jnp.sum(x_wide * x_wide, axis=-1, keepdims=True)
        scale = lax.rsqrt(squares / width + EPSILON)
        gate = (gate_in[at, :] + dot(x, gate_w[...])) * scale
        up = (up_in[at, :] + dot(x, up_w[...])) * scale
        act[at, :] = (gate * (1.0 / (1.0 + jnp.exp(-gate))) * up).astype(BF)
        return carry

    lax.fori_loop(0, 2, step, 0)
    copies[2].wait()
    left = 0
    for out in outs:
        cols = slice(left, left + out.shape[1])
        left += out.shape[1]

        def lower(t, carry, out=out, cols=cols):
            at = pl.ds(pl.multiple_of(t * tile, 16), tile)
            out[at, :] = dot(act[at, :], down_w[:, cols]).astype(BF)
            return carry

        lax.fori_loop(0, 2, lower, 0)


VMEM = pl.BlockSpec(memory_space=pltpu.VMEM)
ANY = pl.BlockSpec(memory_space=pl.ANY)
VMEM_LIMIT = 26 * 1024 * 1024


def gate_up_first(rows, gate_weight, up_weight):
    slots, wide = rows[0].shape
    units = gate_weight.shape[2]
    depth = wide * len(rows)
    return pl.pallas_call(
        functools.partial(gate_up_kernel, len(rows)),
        out_shape=(
            jax.ShapeDtypeStruct((slots, units), F32),
            jax.ShapeDtypeStruct((slots, units), F32),
            jax.ShapeDtypeStruct((slots, 128), F32),
        ),
        in_specs=[VMEM] * len(rows) + [ANY] * 2,
        out_specs=(VMEM,) * 3,
        scratch_shapes=[
            pltpu.VMEM((depth, units), BF),
            pltpu.VMEM((depth, units), BF),
            pltpu.SemaphoreType.DMA((2,)),
        ],
        compiler_params=pltpu.CompilerParams(vmem_limit_bytes=VMEM_LIMIT),
        cost_estimate=pl.CostEstimate(
            flops=4 * slots * depth * units,
            bytes_accessed=4 * depth * units + 2 * slots * depth + 8 * slots * units,
            transcendentals=0,
        ),
    )(*rows, gate_weight, up_weight)


def expert_last(rows, first, gate_weight, up_weight, down_weight, chunks):
    slots, wide = rows.shape
    units, width = down_weight.shape[1:]
    return pl.pallas_call(
        functools.partial(expert_kernel, width),
        out_shape=tuple(jax.ShapeDtypeStruct((slots, width // chunks), BF) for _ in range(chunks)),
        in_specs=[VMEM] * 4 + [ANY] * 3,
        out_specs=(VMEM,) * chunks,
        scratch_shapes=[
            pltpu.VMEM((wide, units), BF),
            pltpu.VMEM((wide, units), BF),
            pltpu.VMEM((units, width), BF),
            pltpu.VMEM((slots, units), BF),
            pltpu.SemaphoreType.DMA((3,)),
        ],
        compiler_params=pltpu.CompilerParams(vmem_limit_bytes=VMEM_LIMIT),
        cost_estimate=pl.CostEstimate(
            flops=4 * slots * wide * units + 2 * slots * units * width,
            bytes_accessed=2 * units * (2 * wide + width) + 2 * slots * (wide + width) + 8 * slots * units,
            transcendentals=slots * units,
        ),
    )(rows, *first, gate_weight, up_weight, down_weight)


def state_kernel(place_ref, lengths_ref, rates_ref, keys, values, out):
    block_len = keys.shape[0]
    heads, size, _ = out.shape
    base = place_ref[0]
    start = jnp.int32(0)
    last_start = start
    for i in range(lengths_ref.shape[0]):
        last_start = jnp.where(start < base + block_len, start, last_start)
        start = start + lengths_ref[i]
    index = lax.broadcasted_iota(jnp.int32, (block_len, size), 0)
    left = (block_len - index).astype(F32)
    same = base + index >= last_start
    dims = (((0,), (0,)), ((), ()))
    for h in range(heads):
        cols = slice(h * size, (h + 1) * size)
        weight = jnp.where(same, jnp.exp(-rates_ref[h] * left), 0.0)
        weighted = keys[:, cols].astype(F32) * weight
        high = weighted.astype(BF)
        low = (weighted - high.astype(F32)).astype(BF)
        v = values[:, cols]
        state = lax.dot_general(high, v, dims, preferred_element_type=F32)
        state = state + lax.dot_general(low, v, dims, preferred_element_type=F32)
        out[h] = state.astype(BF)


def together(values):
    names = list(values)
    joined = lax.optimization_barrier(tuple(values[name] for name in names))
    return dict(zip(names, joined))


def body(
    residual_in,
    queries,
    keys,
    values,
    rates,
    doc_lengths,
    out_weight,
    router,
    gate_weight,
    up_weight,
    down_weight,
    routes,
):
    seq_count = lax.axis_size("seq")
    exp_count = lax.axis_size("exp")
    seq_index = lax.axis_index("seq")
    exp_index = lax.axis_index("exp")
    chips = seq_count // 2
    chip = seq_index // 2
    core = seq_index % 2
    block_len = queries.shape[0]
    head_count = rates.shape[0]
    head_size = queries.shape[1] // head_count
    width = out_weight.shape[1]
    experts = seq_count // 2
    capacity = exp_count * max(1, 2 * block_len // experts * 17 // (16 * exp_count))
    own_count = block_len // exp_count
    local_index = jnp.arange(block_len, dtype=jnp.int32)
    block_base = seq_index * block_len
    position = block_base + local_index
    doc_starts = jnp.cumsum(doc_lengths) - doc_lengths
    doc_of = jnp.sum((doc_starts[None, :] <= position[:, None]).astype(jnp.int32), axis=1) - 1
    query_heads = queries.reshape(block_len, head_count, head_size)
    key_heads = keys.reshape(block_len, head_count, head_size)
    value_heads = values.reshape(block_len, head_count, head_size)

    smem = pl.BlockSpec(memory_space=pltpu.SMEM)
    end_state = pl.pallas_call(
        state_kernel,
        out_shape=jax.ShapeDtypeStruct((head_count, head_size, head_size), BF),
        in_specs=[smem] * 3 + [VMEM] * 2,
        out_specs=VMEM,
    )(block_base.reshape(1), doc_lengths, rates, keys, values)

    half_heads = head_count // 2
    head_at = core * half_heads
    partner_state = lax.ppermute(end_state, "seq", xor_pairs(seq_count, 1))
    mine = lax.dynamic_slice_in_dim(end_state, head_at, half_heads, 0).astype(F32)
    theirs = lax.dynamic_slice_in_dim(partner_state, head_at, half_heads, 0).astype(F32)
    first_state = jnp.where(core == 0, mine, theirs)
    second_state = jnp.where(core == 0, theirs, mine)
    half_rates = lax.dynamic_slice_in_dim(rates, head_at, half_heads, 0)

    def start_at(where):
        return jnp.max(jnp.where(doc_starts <= where, doc_starts, 0))

    chip_base = chip * 2 * block_len
    block_decay = jnp.exp(-half_rates * float(block_len))
    last_start = start_at(chip_base + 2 * block_len - 1)
    keep_first = jnp.where(last_start <= chip_base + block_len - 1, block_decay, 0.0)
    chip_state = (second_state + keep_first[:, None, None] * first_state).astype(BF)
    base_start = start_at(chip_base)
    carried_first = jnp.zeros_like(first_state)
    for step in range(1, chips):
        other_state = lax.ppermute(chip_state, "seq", xor_pairs(seq_count, 2 * step))
        other = jnp.bitwise_xor(chip, step)
        other_end = (other + 1) * 2 * block_len
        usable = (other < chip) & (other_end - 1 >= base_start)
        distance = jnp.maximum(chip_base - other_end, 0).astype(F32)
        weight = jnp.where(usable, jnp.exp(-half_rates * distance), 0.0)
        carried_first = carried_first + weight[:, None, None] * other_state.astype(F32)
    middle = chip_base + block_len
    middle_start = start_at(middle)
    take_first = (middle - 1 >= middle_start).astype(F32)
    take_carried = jnp.where(chip_base - 1 >= middle_start, block_decay, 0.0)
    carried_second = take_first * first_state + take_carried[:, None, None] * carried_first
    carried_first = carried_first.astype(BF)
    carried_second = carried_second.astype(BF)
    carried_mine = jnp.where(core == 0, carried_first, carried_second)
    carried_other = lax.ppermute(
        jnp.where(core == 0, carried_second, carried_first), "seq", xor_pairs(seq_count, 1)
    )
    carried_rounded = jnp.concatenate(
        [
            jnp.where(core == 0, carried_mine, carried_other),
            jnp.where(core == 0, carried_other, carried_mine),
        ],
        axis=0,
    )

    scores = jnp.einsum("thd,uhd->htu", query_heads, key_heads, preferred_element_type=F32)
    lag_steps = local_index[:, None] - local_index[None, :]
    allowed = (lag_steps >= 0) & (doc_of[:, None] == doc_of[None, :])
    decay_mask = jnp.where(
        allowed[None],
        jnp.exp(-rates[:, None, None] * jnp.maximum(lag_steps, 0).astype(F32)[None]),
        0.0,
    )
    scaled_scores = (scores * decay_mask).astype(BF)
    inside_term = jnp.einsum(
        "htu,uhd->thd", scaled_scores, value_heads, preferred_element_type=F32
    )
    carried_term = jnp.einsum(
        "thd,hde->the", query_heads, carried_rounded, preferred_element_type=F32
    )
    carry_scale = (
        jnp.exp(-rates[None, :] * local_index.astype(F32)[:, None])
        * (doc_of == doc_of[0]).astype(F32)[:, None]
    )
    heads_raw = inside_term + carried_term * carry_scale[:, :, None]
    attention = (
        (heads_raw * lax.rsqrt(jnp.mean(heads_raw * heads_raw, axis=-1, keepdims=True) + EPSILON))
        .astype(BF)
        .reshape(block_len, head_count * head_size)
    )
    expert_ids = jnp.arange(experts, dtype=jnp.int32)
    chosen = routes[:, :, None] == expert_ids[None, None, :]
    onehot = jnp.sum(chosen.astype(jnp.int32), axis=1)
    before = (local_index[:, None] > local_index[None, :]).astype(BF)
    rank = jnp.dot(before, onehot.astype(BF), preferred_element_type=F32).astype(jnp.int32)
    slot = jnp.sum(jnp.where(chosen, rank[:, None, :], 0), axis=2)
    group = jnp.bitwise_xor(routes, chip)
    place = group * capacity + slot
    slots = experts * capacity
    slot_ids = jnp.arange(slots, dtype=jnp.int32)
    pick = [(place[:, k][:, None] == slot_ids[None, :]).astype(BF) for k in range(2)]
    spread = jnp.transpose(pick[0] + pick[1])

    chunks = CHUNKS
    wide = width // chunks
    reach = exp_count // 2
    mirror = jnp.minimum(exp_index, exp_count - 1 - exp_index)
    stages = 2 * reach - 1
    hidden = {}
    total = {}
    mine = {}
    theirs = {}

    def project(i):
        cols = slice(i * wide, (i + 1) * wide)
        return jnp.dot(attention, out_weight[:, cols], preferred_element_type=F32).astype(BF)

    part = {0: project(0)}
    for r in range(chunks + stages + 1):
        done = {}
        for side in range(reach - 1):
            inner = r - side
            outer = r - (stages - 1 - side)
            ins = [(side, side + 1), (exp_count - 1 - side, exp_count - 2 - side)]
            outs = [(b, a) for a, b in ins]
            has_in = 0 <= inner < chunks
            has_out = 0 <= outer < chunks
            if not (has_in or has_out):
                continue
            if has_in and has_out:
                load = jnp.where(mirror == side, total.get(inner, part[inner]), hidden[outer])
            else:
                load = total.get(inner, part[inner]) if has_in else hidden[outer]
            done["side", side] = lax.ppermute(
                load, "exp", (ins if has_in else []) + (outs if has_out else [])
            )
        middle = r - (reach - 1)
        if 0 <= middle < chunks:
            done["middle"] = lax.ppermute(
                total.get(middle, part[middle]), "exp", [(reach - 1, reach), (reach, reach - 1)]
            )
        i = r - stages
        if 0 <= i < chunks:
            send = jnp.dot(spread, hidden[i], preferred_element_type=F32).astype(BF)
            done["group", 0] = send[:capacity]
            for g in range(1, chips):
                block = send[g * capacity : (g + 1) * capacity]
                done["group", g] = lax.ppermute(block, "seq", xor_pairs(seq_count, 2 * g))
        i = r - stages - 1
        if 0 <= i < chunks:
            done["theirs"] = lax.ppermute(mine[i], "seq", xor_pairs(seq_count, 1))
        if r == stages + chunks - 1:
            theirs[chunks - 2] = done["theirs"]
            firsts = {
                "mine": gate_up_first([mine[i] for i in range(chunks - 1)], gate_weight, up_weight),
                "theirs": gate_up_first(
                    [theirs[i] for i in range(chunks - 1)], gate_weight, up_weight
                ),
            }
            for side in firsts:
                for k in range(3):
                    done["first", side, k] = firsts[side][k]
        if r == stages + chunks:
            done["lowered"] = expert_last(
                mine[chunks - 1], firsts["mine"], gate_weight, up_weight, down_weight, CHUNKS_BACK
            )
        if r + 1 < chunks:
            done["part"] = project(r + 1)
        done = together(done)
        if "part" in done:
            part[r + 1] = done["part"]
        for side in range(reach - 1):
            inner = r - side
            outer = r - (stages - 1 - side)
            if 0 <= inner < chunks:
                total[inner] = (part[inner].astype(F32) + done["side", side].astype(F32)).astype(BF)
            if 0 <= outer < chunks:
                hidden[outer] = jnp.where(mirror == side, done["side", side], hidden[outer])
        if 0 <= middle < chunks:
            residual = residual_in[:, middle * wide : (middle + 1) * wide].astype(F32)
            whole = total.get(middle, part[middle]).astype(F32) + done["middle"].astype(F32)
            hidden[middle] = (residual + whole).astype(BF)
        if ("group", 0) in done:
            mine[r - stages] = jnp.concatenate([done["group", g] for g in range(chips)], axis=0)
        if "theirs" in done:
            theirs[r - stages - 1] = done["theirs"]
        if ("first", "mine", 0) in done:
            firsts = {
                side: [done["first", side, k] for k in range(3)] for side in ("mine", "theirs")
            }
    kept = done["lowered"]
    partials = expert_last(
        theirs[chunks - 1], firsts["theirs"], gate_weight, up_weight, down_weight, CHUNKS_BACK
    )

    hidden = jnp.concatenate([hidden[i] for i in range(chunks)], axis=1)
    squares = jnp.sum(jnp.square(hidden.astype(F32)), axis=-1, keepdims=True)
    row_scale = lax.rsqrt(squares / width + EPSILON)
    logits = jnp.dot(hidden, router, preferred_element_type=F32) * row_scale
    route_logits = jnp.sum(jnp.where(chosen, logits[:, None, :], 0.0), axis=2)
    route_weight = jax.nn.sigmoid(route_logits - route_logits[:, ::-1])
    own_hidden = lax.dynamic_slice_in_dim(hidden, exp_index * own_count, own_count, 0)

    chunks = CHUNKS_BACK
    wide = width // chunks
    sums = {}
    mixes = {}
    own = {}

    def own_rows(value, index):
        return lax.dynamic_slice_in_dim(value, index * own_count, own_count, 0)

    for r in range(chunks + 2):
        done = {}
        i = r - 1
        if 0 <= i < chunks:
            for g in range(1, chips):
                block = sums[i][g * capacity : (g + 1) * capacity]
                done["table", g] = lax.ppermute(block, "seq", xor_pairs(seq_count, 2 * g))
        i = r - 2
        if 0 <= i < chunks:
            for step in range(exp_count - 1, 0, -1):
                block = own_rows(mixes[i], jnp.bitwise_xor(exp_index, step))
                done["own", step] = lax.ppermute(block, "exp", xor_pairs(exp_count, step))
        for i in range(chunks):
            if r == min(i, 1):
                done["got", i] = lax.ppermute(partials[i], "seq", xor_pairs(seq_count, 1))
        done = together(done)
        for i in range(chunks):
            if ("got", i) in done:
                sums[i] = (
                    kept[i].astype(F32) + done["got", i].astype(F32)
                ).astype(BF)
        i = r - 1
        if 0 <= i < chunks:
            table = jnp.concatenate(
                [sums[i][:capacity]] + [done["table", g] for g in range(1, chips)], axis=0
            )
            mixes[i] = sum(
                jnp.dot(pick[k], table, preferred_element_type=F32) * route_weight[:, k : k + 1]
                for k in range(2)
            ).astype(BF)
        i = r - 2
        if 0 <= i < chunks:
            cols = slice(i * wide, (i + 1) * wide)
            whole = own_hidden[:, cols].astype(F32) + own_rows(mixes[i], exp_index).astype(F32)
            for step in range(1, exp_count):
                whole = whole + done["own", step].astype(F32)
            own[i] = whole.astype(BF)
    return jnp.concatenate([own[i] for i in range(chunks)], axis=1)


def solution(mesh):
    in_specs = (
        P("seq", None),
        P("seq", "exp"),
        P("seq", "exp"),
        P("seq", "exp"),
        P("exp"),
        P(),
        P("exp", None),
        P(),
        P("seq", None, "exp"),
        P("seq", None, "exp"),
        P("seq", "exp", None),
        P("seq", None),
    )
    out_specs = P(("seq", "exp"), None)
    return jax.shard_map(body, mesh=mesh, in_specs=in_specs, out_specs=out_specs, check_vma=False)
```

```python
import functools

import jax
import jax.numpy as jnp
from jax import lax
from jax.experimental import pallas as pl
from jax.experimental.pallas import tpu as pltpu
from jax.sharding import PartitionSpec as P

EPSILON = 1e-06
BF = jnp.bfloat16
F32 = jnp.float32
CHUNKS = 3
CHUNKS_BACK = 3


def xor_pairs(count, step):
    return [(i, i ^ step) for i in range(count)]


def dot(a, b):
    return jnp.dot(a, b, preferred_element_type=F32)


def gate_up_kernel(parts, *refs):
    rows = refs[:parts]
    gate_hbm, up_hbm, gate_out, up_out, squares_out, gate_w, up_w, sems = refs[parts:]
    depth = gate_w.shape[0]
    wide = depth // parts
    copies = [
        pltpu.make_async_copy(hbm.at[0, pl.ds(0, depth)], vmem, sems.at[k])
        for k, (hbm, vmem) in enumerate(((gate_hbm, gate_w), (up_hbm, up_w)))
    ]
    for copy in copies:
        copy.start()
    for copy in copies:
        copy.wait()
    tile = rows[0].shape[0] // 2

    def step(t, carry):
        at = pl.ds(pl.multiple_of(t * tile, 16), tile)
        gate = up = squares = None
        for p in range(parts):
            x = rows[p][at, :]
            x_wide = x.astype(F32)
            depths = slice(p * wide, (p + 1) * wide)
            new = (
                dot(x, gate_w[depths, :]),
                dot(x, up_w[depths, :]),
                jnp.sum(x_wide * x_wide, axis=-1, keepdims=True),
            )
            gate, up, squares = new if p == 0 else (gate + new[0], up + new[1], squares + new[2])
        gate_out[at, :] = gate
        up_out[at, :] = up
        squares_out[at, :] = jnp.broadcast_to(squares, (tile, squares_out.shape[1]))
        return carry

    lax.fori_loop(0, 2, step, 0)


def expert_kernel(
    width, rows, gate_in, up_in, squares_in, gate_hbm, up_hbm, down_hbm, *refs
):
    outs = refs[:-5]
    gate_w, up_w, down_w, act, sems = refs[-5:]
    slots, wide = rows.shape
    copies = [
        pltpu.make_async_copy(hbm, vmem, sems.at[k])
        for k, (hbm, vmem) in enumerate(
            (
                (gate_hbm.at[0, pl.ds(width - wide, wide)], gate_w),
                (up_hbm.at[0, pl.ds(width - wide, wide)], up_w),
                (down_hbm.at[0], down_w),
            )
        )
    ]
    for copy in copies:
        copy.start()
    copies[0].wait()
    copies[1].wait()
    tile = slots // 2

    def step(t, carry):
        at = pl.ds(pl.multiple_of(t * tile, 16), tile)
        x = rows[at, :]
        x_wide = x.astype(F32)
        squares = squares_in[at, :1] + jnp.sum(x_wide * x_wide, axis=-1, keepdims=True)
        scale = lax.rsqrt(squares / width + EPSILON)
        gate = (gate_in[at, :] + dot(x, gate_w[...])) * scale
        up = (up_in[at, :] + dot(x, up_w[...])) * scale
        act[at, :] = (gate * (1.0 / (1.0 + jnp.exp(-gate))) * up).astype(BF)
        return carry

    lax.fori_loop(0, 2, step, 0)
    copies[2].wait()
    left = 0
    for out in outs:
        cols = slice(left, left + out.shape[1])
        left += out.shape[1]

        def lower(t, carry, out=out, cols=cols):
            at = pl.ds(pl.multiple_of(t * tile, 16), tile)
            out[at, :] = dot(act[at, :], down_w[:, cols]).astype(BF)
            return carry

        lax.fori_loop(0, 2, lower, 0)


VMEM = pl.BlockSpec(memory_space=pltpu.VMEM)
ANY = pl.BlockSpec(memory_space=pl.ANY)
VMEM_LIMIT = 26 * 1024 * 1024


def gate_up_first(rows, gate_weight, up_weight):
    slots, wide = rows[0].shape
    units = gate_weight.shape[2]
    depth = wide * len(rows)
    return pl.pallas_call(
        functools.partial(gate_up_kernel, len(rows)),
        out_shape=(
            jax.ShapeDtypeStruct((slots, units), F32),
            jax.ShapeDtypeStruct((slots, units), F32),
            jax.ShapeDtypeStruct((slots, 128), F32),
        ),
        in_specs=[VMEM] * len(rows) + [ANY] * 2,
        out_specs=(VMEM,) * 3,
        scratch_shapes=[
            pltpu.VMEM((depth, units), BF),
            pltpu.VMEM((depth, units), BF),
            pltpu.SemaphoreType.DMA((2,)),
        ],
        compiler_params=pltpu.CompilerParams(vmem_limit_bytes=VMEM_LIMIT),
        cost_estimate=pl.CostEstimate(
            flops=4 * slots * depth * units,
            bytes_accessed=4 * depth * units + 2 * slots * depth + 8 * slots * units,
            transcendentals=0,
        ),
    )(*rows, gate_weight, up_weight)


def expert_last(rows, first, gate_weight, up_weight, down_weight, chunks):
    slots, wide = rows.shape
    units, width = down_weight.shape[1:]
    return pl.pallas_call(
        functools.partial(expert_kernel, width),
        out_shape=tuple(jax.ShapeDtypeStruct((slots, width // chunks), BF) for _ in range(chunks)),
        in_specs=[VMEM] * 4 + [ANY] * 3,
        out_specs=(VMEM,) * chunks,
        scratch_shapes=[
            pltpu.VMEM((wide, units), BF),
            pltpu.VMEM((wide, units), BF),
            pltpu.VMEM((units, width), BF),
            pltpu.VMEM((slots, units), BF),
            pltpu.SemaphoreType.DMA((3,)),
        ],
        compiler_params=pltpu.CompilerParams(vmem_limit_bytes=VMEM_LIMIT),
        cost_estimate=pl.CostEstimate(
            flops=4 * slots * wide * units + 2 * slots * units * width,
            bytes_accessed=2 * units * (2 * wide + width) + 2 * slots * (wide + width) + 8 * slots * units,
            transcendentals=slots * units,
        ),
    )(rows, *first, gate_weight, up_weight, down_weight)


def state_kernel(place_ref, lengths_ref, rates_ref, keys, values, out):
    block_len = keys.shape[0]
    heads, size, _ = out.shape
    base = place_ref[0]
    start = jnp.int32(0)
    last_start = start
    for i in range(lengths_ref.shape[0]):
        last_start = jnp.where(start < base + block_len, start, last_start)
        start = start + lengths_ref[i]
    index = lax.broadcasted_iota(jnp.int32, (block_len, size), 0)
    left = (block_len - index).astype(F32)
    same = base + index >= last_start
    dims = (((0,), (0,)), ((), ()))
    for h in range(heads):
        cols = slice(h * size, (h + 1) * size)
        weight = jnp.where(same, jnp.exp(-rates_ref[h] * left), 0.0)
        weighted = keys[:, cols].astype(F32) * weight
        high = weighted.astype(BF)
        low = (weighted - high.astype(F32)).astype(BF)
        v = values[:, cols]
        state = lax.dot_general(high, v, dims, preferred_element_type=F32)
        state = state + lax.dot_general(low, v, dims, preferred_element_type=F32)
        out[h] = state.astype(BF)


def inside_kernel(place_ref, lengths_ref, rates_ref, queries, keys, values, out, same_out):
    block_len = queries.shape[0]
    heads = rates_ref.shape[0]
    size = queries.shape[1] // heads
    base = place_ref[0]
    index = lax.broadcasted_iota(jnp.int32, (block_len, 1), 0)
    start = jnp.int32(0)
    doc_start = jnp.zeros((block_len, 1), jnp.int32)
    for i in range(lengths_ref.shape[0]):
        doc_start = jnp.where(base + index >= start, start, doc_start)
        start = start + lengths_ref[i]
    row = lax.broadcasted_iota(jnp.int32, (block_len, block_len), 0)
    col = lax.broadcasted_iota(jnp.int32, (block_len, block_len), 1)
    allowed = (col <= row) & (base + col >= doc_start)
    lag = jnp.maximum(row - col, 0).astype(F32)
    same_out[...] = jnp.broadcast_to(jnp.where(doc_start <= base, 1.0, 0.0), same_out.shape)
    for h in range(heads):
        cols = slice(h * size, (h + 1) * size)
        scores = lax.dot_general(
            queries[:, cols], keys[:, cols], (((1,), (1,)), ((), ())), preferred_element_type=F32
        )
        decay = jnp.where(allowed, jnp.exp(-rates_ref[h] * lag), 0.0)
        out[:, cols] = dot((scores * decay).astype(BF), values[:, cols])


def attention_kernel(rates_ref, queries, inside, same, carried, out):
    block_len = queries.shape[0]
    heads, size, _ = carried.shape
    index = lax.broadcasted_iota(jnp.int32, (block_len, size), 0).astype(F32)
    for h in range(heads):
        cols = slice(h * size, (h + 1) * size)
        scale = jnp.exp(-rates_ref[h] * index) * same[...]
        raw = inside[:, cols] + dot(queries[:, cols], carried[h]) * scale
        mean = jnp.mean(raw * raw, axis=-1, keepdims=True)
        out[:, cols] = (raw * lax.rsqrt(mean + EPSILON)).astype(BF)


def together(values):
    names = list(values)
    joined = lax.optimization_barrier(tuple(values[name] for name in names))
    return dict(zip(names, joined))


def body(
    residual_in,
    queries,
    keys,
    values,
    rates,
    doc_lengths,
    out_weight,
    router,
    gate_weight,
    up_weight,
    down_weight,
    routes,
):
    seq_count = lax.axis_size("seq")
    exp_count = lax.axis_size("exp")
    seq_index = lax.axis_index("seq")
    exp_index = lax.axis_index("exp")
    chips = seq_count // 2
    chip = seq_index // 2
    core = seq_index % 2
    block_len = queries.shape[0]
    head_count = rates.shape[0]
    head_size = queries.shape[1] // head_count
    width = out_weight.shape[1]
    experts = seq_count // 2
    capacity = exp_count * max(1, 2 * block_len // experts * 17 // (16 * exp_count))
    own_count = block_len // exp_count
    local_index = jnp.arange(block_len, dtype=jnp.int32)
    block_base = seq_index * block_len
    position = block_base + local_index
    doc_starts = jnp.cumsum(doc_lengths) - doc_lengths
    doc_of = jnp.sum((doc_starts[None, :] <= position[:, None]).astype(jnp.int32), axis=1) - 1
    query_heads = queries.reshape(block_len, head_count, head_size)
    key_heads = keys.reshape(block_len, head_count, head_size)
    value_heads = values.reshape(block_len, head_count, head_size)

    smem = pl.BlockSpec(memory_space=pltpu.SMEM)
    end_state = pl.pallas_call(
        state_kernel,
        out_shape=jax.ShapeDtypeStruct((head_count, head_size, head_size), BF),
        in_specs=[smem] * 3 + [VMEM] * 2,
        out_specs=VMEM,
    )(block_base.reshape(1), doc_lengths, rates, keys, values)

    half_heads = head_count // 2
    head_at = core * half_heads
    partner_state = lax.ppermute(end_state, "seq", xor_pairs(seq_count, 1))
    mine = lax.dynamic_slice_in_dim(end_state, head_at, half_heads, 0).astype(F32)
    theirs = lax.dynamic_slice_in_dim(partner_state, head_at, half_heads, 0).astype(F32)
    first_state = jnp.where(core == 0, mine, theirs)
    second_state = jnp.where(core == 0, theirs, mine)
    half_rates = lax.dynamic_slice_in_dim(rates, head_at, half_heads, 0)

    def start_at(where):
        return jnp.max(jnp.where(doc_starts <= where, doc_starts, 0))

    chip_base = chip * 2 * block_len
    block_decay = jnp.exp(-half_rates * float(block_len))
    last_start = start_at(chip_base + 2 * block_len - 1)
    keep_first = jnp.where(last_start <= chip_base + block_len - 1, block_decay, 0.0)
    chip_state = (second_state + keep_first[:, None, None] * first_state).astype(BF)
    base_start = start_at(chip_base)
    carried_first = jnp.zeros_like(first_state)
    for step in range(1, chips):
        other_state = lax.ppermute(chip_state, "seq", xor_pairs(seq_count, 2 * step))
        other = jnp.bitwise_xor(chip, step)
        other_end = (other + 1) * 2 * block_len
        usable = (other < chip) & (other_end - 1 >= base_start)
        distance = jnp.maximum(chip_base - other_end, 0).astype(F32)
        weight = jnp.where(usable, jnp.exp(-half_rates * distance), 0.0)
        carried_first = carried_first + weight[:, None, None] * other_state.astype(F32)
    middle = chip_base + block_len
    middle_start = start_at(middle)
    take_first = (middle - 1 >= middle_start).astype(F32)
    take_carried = jnp.where(chip_base - 1 >= middle_start, block_decay, 0.0)
    carried_second = take_first * first_state + take_carried[:, None, None] * carried_first
    inside, same = pl.pallas_call(
        inside_kernel,
        out_shape=(
            jax.ShapeDtypeStruct(queries.shape, F32),
            jax.ShapeDtypeStruct((block_len, head_size), F32),
        ),
        in_specs=[smem] * 3 + [VMEM] * 3,
        out_specs=(VMEM, VMEM),
        cost_estimate=pl.CostEstimate(
            flops=4 * block_len * block_len * queries.shape[1],
            bytes_accessed=10 * block_len * queries.shape[1],
            transcendentals=head_count * block_len * block_len,
        ),
    )(block_base.reshape(1), doc_lengths, rates, queries, keys, values)
    carried_first, inside = lax.optimization_barrier((carried_first, inside))
    carried_first = carried_first.astype(BF)
    carried_second = carried_second.astype(BF)
    carried_mine = jnp.where(core == 0, carried_first, carried_second)
    carried_other = lax.ppermute(
        jnp.where(core == 0, carried_second, carried_first), "seq", xor_pairs(seq_count, 1)
    )
    carried_rounded = jnp.concatenate(
        [
            jnp.where(core == 0, carried_mine, carried_other),
            jnp.where(core == 0, carried_other, carried_mine),
        ],
        axis=0,
    )

    attention = pl.pallas_call(
        attention_kernel,
        out_shape=jax.ShapeDtypeStruct(queries.shape, BF),
        in_specs=[smem] + [VMEM] * 4,
        out_specs=VMEM,
    )(rates, queries, inside, same, carried_rounded)

    expert_ids = jnp.arange(experts, dtype=jnp.int32)
    chosen = routes[:, :, None] == expert_ids[None, None, :]
    onehot = jnp.sum(chosen.astype(jnp.int32), axis=1)
    before = (local_index[:, None] > local_index[None, :]).astype(BF)
    rank = jnp.dot(before, onehot.astype(BF), preferred_element_type=F32).astype(jnp.int32)
    slot = jnp.sum(jnp.where(chosen, rank[:, None, :], 0), axis=2)
    group = jnp.bitwise_xor(routes, chip)
    place = group * capacity + slot
    slots = experts * capacity
    slot_ids = jnp.arange(slots, dtype=jnp.int32)
    pick = [(place[:, k][:, None] == slot_ids[None, :]).astype(BF) for k in range(2)]
    spread = jnp.transpose(pick[0] + pick[1])

    chunks = CHUNKS
    wide = width // chunks
    reach = exp_count // 2
    mirror = jnp.minimum(exp_index, exp_count - 1 - exp_index)
    stages = 2 * reach - 1
    hidden = {}
    total = {}
    mine = {}
    theirs = {}

    def project(i):
        cols = slice(i * wide, (i + 1) * wide)
        return jnp.dot(attention, out_weight[:, cols], preferred_element_type=F32).astype(BF)

    part = {0: project(0)}
    for r in range(chunks + stages + 1):
        done = {}
        for side in range(reach - 1):
            inner = r - side
            outer = r - (stages - 1 - side)
            ins = [(side, side + 1), (exp_count - 1 - side, exp_count - 2 - side)]
            outs = [(b, a) for a, b in ins]
            has_in = 0 <= inner < chunks
            has_out = 0 <= outer < chunks
            if not (has_in or has_out):
                continue
            if has_in and has_out:
                load = jnp.where(mirror == side, total.get(inner, part[inner]), hidden[outer])
            else:
                load = total.get(inner, part[inner]) if has_in else hidden[outer]
            done["side", side] = lax.ppermute(
                load, "exp", (ins if has_in else []) + (outs if has_out else [])
            )
        middle = r - (reach - 1)
        if 0 <= middle < chunks:
            done["middle"] = lax.ppermute(
                total.get(middle, part[middle]), "exp", [(reach - 1, reach), (reach, reach - 1)]
            )
        i = r - stages
        if 0 <= i < chunks:
            send = jnp.dot(spread, hidden[i], preferred_element_type=F32).astype(BF)
            done["group", 0] = send[:capacity]
            for g in range(1, chips):
                block = send[g * capacity : (g + 1) * capacity]
                done["group", g] = lax.ppermute(block, "seq", xor_pairs(seq_count, 2 * g))
        i = r - stages - 1
        if 0 <= i < chunks:
            done["theirs"] = lax.ppermute(mine[i], "seq", xor_pairs(seq_count, 1))
        if r == stages + chunks - 1:
            theirs[chunks - 2] = done["theirs"]
            firsts = {
                "mine": gate_up_first([mine[i] for i in range(chunks - 1)], gate_weight, up_weight),
                "theirs": gate_up_first(
                    [theirs[i] for i in range(chunks - 1)], gate_weight, up_weight
                ),
            }
            for side in firsts:
                for k in range(3):
                    done["first", side, k] = firsts[side][k]
        if r == stages + chunks:
            done["lowered"] = expert_last(
                mine[chunks - 1], firsts["mine"], gate_weight, up_weight, down_weight, CHUNKS_BACK
            )
        if r + 1 < chunks:
            done["part"] = project(r + 1)
        done = together(done)
        if "part" in done:
            part[r + 1] = done["part"]
        for side in range(reach - 1):
            inner = r - side
            outer = r - (stages - 1 - side)
            if 0 <= inner < chunks:
                total[inner] = (part[inner].astype(F32) + done["side", side].astype(F32)).astype(BF)
            if 0 <= outer < chunks:
                hidden[outer] = jnp.where(mirror == side, done["side", side], hidden[outer])
        if 0 <= middle < chunks:
            residual = residual_in[:, middle * wide : (middle + 1) * wide].astype(F32)
            whole = total.get(middle, part[middle]).astype(F32) + done["middle"].astype(F32)
            hidden[middle] = (residual + whole).astype(BF)
        if ("group", 0) in done:
            mine[r - stages] = jnp.concatenate([done["group", g] for g in range(chips)], axis=0)
        if "theirs" in done:
            theirs[r - stages - 1] = done["theirs"]
        if ("first", "mine", 0) in done:
            firsts = {
                side: [done["first", side, k] for k in range(3)] for side in ("mine", "theirs")
            }
    kept = done["lowered"]
    partials = expert_last(
        theirs[chunks - 1], firsts["theirs"], gate_weight, up_weight, down_weight, CHUNKS_BACK
    )

    hidden = jnp.concatenate([hidden[i] for i in range(chunks)], axis=1)
    squares = jnp.sum(jnp.square(hidden.astype(F32)), axis=-1, keepdims=True)
    row_scale = lax.rsqrt(squares / width + EPSILON)
    logits = jnp.dot(hidden, router, preferred_element_type=F32) * row_scale
    route_logits = jnp.sum(jnp.where(chosen, logits[:, None, :], 0.0), axis=2)
    route_weight = jax.nn.sigmoid(route_logits - route_logits[:, ::-1])
    own_hidden = lax.dynamic_slice_in_dim(hidden, exp_index * own_count, own_count, 0)

    chunks = CHUNKS_BACK
    wide = width // chunks
    sums = {}
    mixes = {}
    own = {}

    def own_rows(value, index):
        return lax.dynamic_slice_in_dim(value, index * own_count, own_count, 0)

    for r in range(chunks + 2):
        done = {}
        i = r - 1
        if 0 <= i < chunks:
            for g in range(1, chips):
                block = sums[i][g * capacity : (g + 1) * capacity]
                done["table", g] = lax.ppermute(block, "seq", xor_pairs(seq_count, 2 * g))
        i = r - 2
        if 0 <= i < chunks:
            for step in range(exp_count - 1, 0, -1):
                block = own_rows(mixes[i], jnp.bitwise_xor(exp_index, step))
                done["own", step] = lax.ppermute(block, "exp", xor_pairs(exp_count, step))
        for i in range(chunks):
            if r == min(i, 1):
                done["got", i] = lax.ppermute(partials[i], "seq", xor_pairs(seq_count, 1))
        done = together(done)
        for i in range(chunks):
            if ("got", i) in done:
                sums[i] = (
                    kept[i].astype(F32) + done["got", i].astype(F32)
                ).astype(BF)
        i = r - 1
        if 0 <= i < chunks:
            table = jnp.concatenate(
                [sums[i][:capacity]] + [done["table", g] for g in range(1, chips)], axis=0
            )
            mixes[i] = sum(
                jnp.dot(pick[k], table, preferred_element_type=F32) * route_weight[:, k : k + 1]
                for k in range(2)
            ).astype(BF)
        i = r - 2
        if 0 <= i < chunks:
            cols = slice(i * wide, (i + 1) * wide)
            whole = own_hidden[:, cols].astype(F32) + own_rows(mixes[i], exp_index).astype(F32)
            for step in range(1, exp_count):
                whole = whole + done["own", step].astype(F32)
            own[i] = whole.astype(BF)
    return jnp.concatenate([own[i] for i in range(chunks)], axis=1)


def solution(mesh):
    in_specs = (
        P("seq", None),
        P("seq", "exp"),
        P("seq", "exp"),
        P("seq", "exp"),
        P("exp"),
        P(),
        P("exp", None),
        P(),
        P("seq", None, "exp"),
        P("seq", None, "exp"),
        P("seq", "exp", None),
        P("seq", None),
    )
    out_specs = P(("seq", "exp"), None)
    return jax.shard_map(body, mesh=mesh, in_specs=in_specs, out_specs=out_specs, check_vma=False)
```
